256 devices in a mesh: src: 8 (over z), space: 32 (over x, y, core).
Axes of the slice: x: 4, y: 4, z: 8, core: 2. Of those that a mesh axis runs over, the one named last changes fastest.
Arguments:
- background: float32 [2, 8, 3, 64, 32, 128], P(None, 'src', None, 'space'), may hold values from -6 to 6
- warm_start: float32 [2, 8, 3, 64, 32, 128], P(None, 'src', None, 'space'), may hold values from -0.15625 to 0.15625
- conductivity: float32 [64, 32, 128], P('space'), may hold values from 0.3 to 3
- frequencies: float32 [8], replicated, may hold values from 0.1 to 1
- pair_freq: int32 [8], P('src'), may hold values from 0 to 7
- weighted_residual: float32 [2, 8, 4096], P(None, 'src', 'space'), may hold values from -6 to 6
- datum_layer_index: int32 [4096, 1], replicated, may hold values from 0 to 31; in each aligned block of 128 rows (0 to 127, 128 to 255, ...) at most 8 rows name the same one
- receiver_flat_cell: int32 [4096], replicated, may hold values from 0 to 8191
- receiver_component: int32 [4096], replicated, may hold values from 0 to 2
Outputs:
- adjoint: float32 [2, 8, 3, 64, 32, 128], P(None, 'src', None, 'space')
- gradient: float32 [64, 32, 128], P('space', 'src')
The draws below stay inside these ranges and needn't reach their ends.
Inputs may be any that keep to these rules, and one draw needn't show every extreme that they name: `datum_layer_index`: among the 128 measurements of each aligned block (the measurements of one device), no slab is named by more than 8 of them, a bound that some block reaches.
All inputs are finite; a program needn't handle non-finite values.
Results may differ from the reference program's by a relative error of at most 0.0001.
Values sent between devices are 32-bit elements; how exact they have to be, the bound alone decides.
No kernel may reach another device: no remote copies, remote signals or barrier semaphores. Data moves between devices by JAX's collectives and lax.ppermute only.
A program may use at most 64 MiB of HBM per device.

```python
import math
import jax
import jax.numpy as jnp
import numpy as np
from jax import lax

SLAB_PLANES = 2
CELLS_SECOND = 32
CELLS_THIRD = 128
DATA_PER_SITE = 128
NFREQ = 8
ITERS = 4
SOURCE_FREQ_PAIRS = 8
NX = 64
DATUM_TOTAL = 4096
LAYER_DATUM_CAP = 8
N_SPACE = 32


def plant(result, rng, low, largest):
    longest = result.shape.index(max(result.shape))
    spots = []
    for shift in (0, 1):
        where = [jax.random.randint(jax.random.fold_in(rng, axis), (), 0, length) for axis, length in enumerate(result.shape)]
        where[longest] = (where[longest] + shift) % result.shape[longest]
        spots.append(tuple(where))
    return result.at[spots[0]].set(low).at[spots[1]].set(largest)


def shard_levels(rng, dims, pieces, least, largest):
    level = 1.0
    for position, parts in pieces:
        heights = jax.random.uniform(jax.random.fold_in(jax.random.fold_in(rng, 6), position), (parts,), jnp.float32, least / len(pieces), largest / len(pieces))
        level = level * jnp.repeat(jnp.exp(heights), dims[position] // parts).reshape((-1,) + (1,) * (len(dims) - 1 - position))
    return level


def shared_out(key, own, number, rows, count, top, most, slope):
    ranking = jax.random.permutation(key, count)
    packed, usual = portions_of(count, rows * top, most, slope, True), portions_of(count, rows * top, most, slope, False)
    places = jnp.arange(count)

    def named(sizes, rotation):
        used = int((sizes > 0).sum())
        fixed = max(1, used // 4)
        passed = fixed + (places - fixed + rotation * (used - fixed)) % max(1, count - fixed)
        return jnp.zeros((count,), jnp.int32).at[ranking[jnp.where(places < fixed, places, passed)]].set(jnp.asarray(sizes, jnp.int32))

    sizes = jnp.where(number % 4 == 0, named(packed, number // 4), named(usual, number - number // 4 - 1))
    mixed = jax.random.permutation(jax.random.fold_in(own, 3), count)
    donor, sink = mixed[0:count // 2 * 2:2], mixed[1:count // 2 * 2:2]
    slack = jnp.minimum(sizes[donor] - 1, most - sizes[sink]) // 2
    slack = jnp.where((donor == ranking[0]) | (sink == ranking[0]) | (sizes[sink] == 0), 0, jnp.maximum(slack, 0))
    passed = jax.random.randint(jax.random.fold_in(own, 4), (count // 2,), 0, 1 << 20) % (slack + 1)
    sizes = sizes.at[donor].add(-passed).at[sink].add(passed)
    members = jnp.searchsorted(jnp.cumsum(sizes), jnp.arange(rows * top), side="right").astype(jnp.int32)
    grid = members.reshape(top, rows).T
    grid = grid[jax.random.permutation(jax.random.fold_in(own, 1), rows)]
    rotation = jax.random.randint(jax.random.fold_in(own, 2), (rows, 1), 0, top)
    return jnp.take_along_axis(grid, (jnp.arange(top)[None, :] + rotation) % top, axis=1)


def portions_of(amount, total, bound, skew, full):
    weights = [(1 << 20) // math.isqrt(rank ** skew) + 1 for rank in range(1, amount + 1)]
    largest = bound if full else min(bound, max(-(-total // amount), total * weights[0] // sum(weights)))
    least = 1 if total - largest >= amount - 1 else 0
    counts, surplus = [largest] + [least] * (amount - 1), total - largest - least * (amount - 1)
    while surplus > 0:
        free = [i for i in range(1, amount) if counts[i] < largest] or [i for i in range(1, amount) if counts[i] < bound]
        mass, left = sum([weights[i] for i in free]), surplus
        for i in free:
            more = min(bound - counts[i], max(1, left * weights[i] // mass), surplus)
            counts[i] = counts[i] + more
            surplus = surplus - more
    return np.array(counts)


def normal_values(own_key, dims, spread, limit, cuts=(), dtype=jnp.bfloat16):
    drawn = spread * jax.random.normal(own_key, dims, jnp.float32)
    if cuts:
        drawn = drawn * shard_levels(own_key, dims, cuts, -0.22, 0.18)
    return jnp.clip(drawn, -limit, limit).astype(dtype)


def setup_inputs(seed: int = 0) -> dict:
    splits = jax.random.split(jax.random.key(seed), 10)
    background = normal_values(splits[0], (2, SOURCE_FREQ_PAIRS, 3, NX, CELLS_SECOND, CELLS_THIRD), 1.0, 6.0, ((1, 8), (3, 32)), jnp.float32)
    warm_start = normal_values(splits[1], (2, SOURCE_FREQ_PAIRS, 3, NX, CELLS_SECOND, CELLS_THIRD), 0.01, 0.15625, ((1, 8), (3, 32)), jnp.float32)
    conductivity = jnp.clip(jnp.exp(math.log(3.0) - 2.3025851 * jax.random.uniform(splits[2], (NX, CELLS_SECOND, CELLS_THIRD), jnp.float32) ** shard_levels(splits[2], (NX, CELLS_SECOND, CELLS_THIRD), ((0, 32),), -0.2, 0.2)), 0.3, 3.0)
    frequencies = jnp.clip(jnp.exp(jax.random.uniform(splits[3], (NFREQ,), jnp.float32, math.log(0.1), math.log(1.0))), 0.1, 1.0)
    pair_freq = plant(jax.random.randint(splits[4], (SOURCE_FREQ_PAIRS,), 0, NFREQ), jax.random.fold_in(splits[4], 1), 0, NFREQ - 1).astype(jnp.int32)
    weighted_residual = normal_values(splits[5], (2, SOURCE_FREQ_PAIRS, DATUM_TOTAL), 1.0, 6.0, ((1, 8), (2, 32)), jnp.float32)
    datum_layer_index_keys = jax.random.split(jax.random.fold_in(splits[6], 1), DATUM_TOTAL // DATA_PER_SITE)
    datum_layer_index_turns = jax.random.permutation(jax.random.fold_in(splits[6], 3), DATUM_TOTAL // DATA_PER_SITE)
    datum_layer_index = jax.vmap(lambda own, number: shared_out(jax.random.fold_in(splits[6], 2), own, number, DATA_PER_SITE, N_SPACE, 1, LAYER_DATUM_CAP, 2))(datum_layer_index_keys, datum_layer_index_turns).reshape((DATUM_TOTAL, 1))
    receiver_flat_cell = plant(jax.random.randint(splits[7], (DATUM_TOTAL,), 0, SLAB_PLANES * CELLS_SECOND * CELLS_THIRD), jax.random.fold_in(splits[7], 1), 0, (SLAB_PLANES * CELLS_SECOND * CELLS_THIRD) - 1).astype(jnp.int32)
    receiver_component = plant(jax.random.randint(splits[8], (DATUM_TOTAL,), 0, 3), jax.random.fold_in(splits[8], 1), 0, 2).astype(jnp.int32)
    return dict(background=background, warm_start=warm_start, conductivity=conductivity, frequencies=frequencies, pair_freq=pair_freq, weighted_residual=weighted_residual, datum_layer_index=datum_layer_index, receiver_flat_cell=receiver_flat_cell, receiver_component=receiver_component)


def diff_forward(field, spatial):
    base = field[..., :-1, :-1, :-1]
    if spatial == 0:
        return field[..., 1:, :-1, :-1] - base
    if spatial == 1:
        return field[..., :-1, 1:, :-1] - base
    return field[..., :-1, :-1, 1:] - base


def diff_backward(field, spatial):
    base = field[..., 1:, 1:, 1:]
    if spatial == 0:
        return base - field[..., :-1, 1:, 1:]
    if spatial == 1:
        return base - field[..., 1:, :-1, 1:]
    return base - field[..., 1:, 1:, :-1]


def curl_forward(padded):
    comp_x = padded[..., 0, :, :, :]
    comp_y = padded[..., 1, :, :, :]
    comp_z = padded[..., 2, :, :, :]
    mag_x = diff_forward(comp_z, 1) - diff_forward(comp_y, 2)
    mag_y = diff_forward(comp_x, 2) - diff_forward(comp_z, 0)
    mag_z = diff_forward(comp_y, 0) - diff_forward(comp_x, 1)
    return jnp.stack([mag_x, mag_y, mag_z], axis=-4)


def curl_backward(magnetic):
    mag_x = magnetic[..., 0, :, :, :]
    mag_y = magnetic[..., 1, :, :, :]
    mag_z = magnetic[..., 2, :, :, :]
    out_x = diff_backward(mag_z, 1) - diff_backward(mag_y, 2)
    out_y = diff_backward(mag_x, 2) - diff_backward(mag_z, 0)
    out_z = diff_backward(mag_y, 0) - diff_backward(mag_x, 1)
    return jnp.stack([out_x, out_y, out_z], axis=-4)


def operate(field, damping):
    padded = jnp.pad(field, ((0, 0), (0, 0), (1, 1), (1, 1), (1, 1)))
    curled = curl_backward(curl_forward(padded))
    return jnp.stack([curled[0] - damping * field[1], curled[1] + damping * field[0]])


def inner(first_vec, second_vec):
    real_part = jnp.sum(first_vec[0] * second_vec[0] + first_vec[1] * second_vec[1])
    quadrature_share = jnp.sum(first_vec[0] * second_vec[1] - first_vec[1] * second_vec[0])
    return real_part, quadrature_share


def scaled(coef_re, coef_im, field):
    return jnp.stack([coef_re * field[0] - coef_im * field[1], coef_re * field[1] + coef_im * field[0]])


def solve_pair(start, source, damping):
    adjoint = start
    residual = source - operate(adjoint, damping)
    direction = residual
    mapped = operate(direction, damping)
    for sweep in range(ITERS):
        mixed_product_real, cross_im = inner(mapped, residual)
        projected_magnitude = jnp.sum(mapped * mapped)
        alpha_re = mixed_product_real / projected_magnitude
        alpha_im = cross_im / projected_magnitude
        adjoint = adjoint + scaled(alpha_re, alpha_im, direction)
        residual = residual - scaled(alpha_re, alpha_im, mapped)
        if sweep + 1 < ITERS:
            fresh = operate(residual, damping)
            turn_re, turn_im = inner(mapped, fresh)
            beta_re = -turn_re / projected_magnitude
            beta_im = -turn_im / projected_magnitude
            direction = residual + scaled(beta_re, beta_im, direction)
            mapped = fresh + scaled(beta_re, beta_im, mapped)
    return adjoint


def reference(background, warm_start, conductivity, frequencies, pair_freq, weighted_residual, datum_layer_index, receiver_flat_cell, receiver_component):
    total_cells = NX * CELLS_SECOND * CELLS_THIRD
    slab_cells = SLAB_PLANES * CELLS_SECOND * CELLS_THIRD
    target = (receiver_component * total_cells + datum_layer_index[:, 0] * slab_cells + receiver_flat_cell).astype(jnp.int32)
    flat_src = jnp.zeros((2, SOURCE_FREQ_PAIRS, 3 * total_cells), jnp.float32).at[:, :, target].add(weighted_residual)
    source = flat_src.reshape(2, SOURCE_FREQ_PAIRS, 3, NX, CELLS_SECOND, CELLS_THIRD)
    wave_k = frequencies[pair_freq.astype(jnp.int32)]
    items = (jnp.moveaxis(warm_start, 1, 0), jnp.moveaxis(source, 1, 0), jnp.moveaxis(background, 1, 0), wave_k)

    def one_pair(total, item):
        start, pair_src, pair_bg, pair_k = item
        adjoint = solve_pair(start, pair_src, pair_k * conductivity)
        total = total + pair_k * jnp.sum(adjoint[0] * pair_bg[1] + adjoint[1] * pair_bg[0], axis=0)
        return total, adjoint

    gradient, adjoints = lax.scan(one_pair, jnp.zeros((NX, CELLS_SECOND, CELLS_THIRD), jnp.float32), items)
    return jnp.moveaxis(adjoints, 0, 1), gradient
```

```python
import functools

import jax
import jax.numpy as jnp
from jax import lax
from jax.experimental import pallas as pl
from jax.experimental.pallas import tpu as pltpu
from jax.sharding import PartitionSpec as P

F32 = jnp.float32
SLABS = (-2, -1, 0, 1, 2, 3)
ROWS, LANES = 32, 128
BLK = (8, 128)
CAP = 8
VMEM_BYTES = 40 * 1024 * 1024


def spec(space=pltpu.VMEM):
    return pl.BlockSpec(memory_space=space)


def iota(shape, axis):
    return lax.broadcasted_iota(jnp.int32, shape, axis)


def two_sum(a, b):
    s = a + b
    t = s - a
    return s, (a - (s - t)) + (b - t)


def split(a):
    t = a * F32(4097.0)
    high = t - (t - a)
    return high, a - high


def product_error(p, a, b):
    (ah, al), (bh, bl) = a, b
    return ((ah * bh - p) + ah * bl + al * bh) + al * bl


def pair_add(a, b):
    s, e = two_sum(a[0], b[0])
    e = e + (a[1] + b[1])
    h = s + e
    return h, e - (h - s)


def pair_scale(a, c):
    p = a[0] * c
    e = product_error(p, split(a[0]), split(c)) + a[1] * c
    h = p + e
    return h, e - (h - p)


def negate(a):
    return tuple(-v for v in a)


def total(terms):
    return functools.reduce(pair_add, terms)


def mix_re(g, v):
    return pair_add(pair_scale(g[0], v[0]), negate(pair_scale(g[1], v[1])))


def mix(g, v):
    return mix_re(g, v), pair_add(pair_scale(g[0], v[1]), pair_scale(g[1], v[0]))


def csum(terms):
    return total([t[0] for t in terms]), total([t[1] for t in terms])


def conj(g):
    return g[0], negate(g[1])


def cneg(v):
    return -v[0], -v[1]


def cmul(a, b):
    return a[0] * b[0] - a[1] * b[1], a[0] * b[1] + a[1] * b[0]


def over(g, den):
    return g[0][0] / den, g[1][0] / den


def y_next(e):
    return jnp.where(iota(e.shape, 0) == ROWS - 1, F32(0), pltpu.roll(e, ROWS - 1, 0))


def z_next(e):
    return jnp.where(iota(e.shape, 1) == LANES - 1, F32(0), pltpu.roll(e, LANES - 1, 1))


def y_prev(h, first):
    return jnp.where(iota(h.shape, 0) == 0, first, pltpu.roll(h, 1, 0))


def z_prev(h, first):
    return jnp.where(iota(h.shape, 1) == 0, first, pltpu.roll(h, 1, 1))


def curl_curl(field, part, at, above, below):
    ex, ey, ez = (field[3 * part + c, at] for c in range(3))
    ey_up, ez_up = (field[3 * part + c, at + 1] * above for c in (1, 2))
    ex_dn, ey_dn, ez_dn = (field[3 * part + c, at - 1] * below for c in range(3))
    hx = (y_next(ez) - ez) - (z_next(ey) - ey)
    hy = (z_next(ex) - ex) - (ez_up - ez)
    hz = (ey_up - ey) - (y_next(ex) - ex)
    hy_dn = (z_next(ex_dn) - ex_dn) - (ez - ez_dn)
    hz_dn = (ey - ey_dn) - (y_next(ex_dn) - ex_dn)
    return (
        (hz - y_prev(hz, -ex)) - (hy - z_prev(hy, ex)),
        (hx - z_prev(hx, -ey)) - (hz - hz_dn),
        (hy - hy_dn) - (hx - y_prev(hx, ez)),
    )


def apply(me, field, damping, first, low, high, store):
    @pl.loop(low, high)
    def _(at):
        grid_plane = lax.rem(2 * me + first + at + 64, 64)
        above = jnp.where(grid_plane == 63, F32(0), F32(1))
        below = jnp.where(grid_plane == 0, F32(0), F32(1))
        damp = damping[at]
        real = curl_curl(field, 0, at, above, below)
        for c in range(3):
            store(0, c, at, real[c] - damp * field[3 + c, at])
        imag = curl_curl(field, 1, at, above, below)
        for c in range(3):
            store(1, c, at, imag[c] + damp * field[c, at])


def gram(fields, pairs, out, size=4):
    sums = []
    for first in range(0, len(pairs), size):
        group = pairs[first : first + size]
        used = sorted({k for pair in group for k in pair})
        count = sum(1 if i == j else 2 for i, j in group)

        def body(step, acc, group=group, used=used):
            comp, rest = step // 8, lax.rem(step, 8)
            plane, row = rest // 4, pl.multiple_of(lax.rem(rest, 4) * 8, 8)
            values = {}
            for k in used:
                ref, start = fields[k]
                for part in range(2):
                    v = ref[3 * part + comp, start + plane, pl.ds(row, 8), :]
                    values[k, part] = v, split(v)

            def add(acc, a, b, minus=False):
                p = a[0] * b[0]
                e = product_error(p, a[1], b[1])
                p, e = (-p, -e) if minus else (p, e)
                s, lost = two_sum(acc[0], p)
                return s, acc[1] + (lost + e)

            new = []
            for i, j in group:
                re = acc[len(new)]
                re = add(re, values[i, 0], values[j, 0])
                new.append(add(re, values[i, 1], values[j, 1]))
                if i != j:
                    im = acc[len(new)]
                    im = add(im, values[i, 0], values[j, 1])
                    new.append(add(im, values[i, 1], values[j, 0], minus=True))
            return tuple(new)

        zero = jnp.zeros(BLK, F32)
        sums += list(lax.fori_loop(0, 24, body, tuple((zero, zero) for _ in range(count))))
    packed = []
    for first in range(0, len(sums), 8):
        high = low = jnp.zeros(BLK, F32)
        for k, s in enumerate(sums[first : first + 8]):
            for shift in (4, 2, 1):
                s = pair_add(s, tuple(pltpu.roll(v, shift, 0) for v in s))
            here = iota(BLK, 0) == k
            high, low = jnp.where(here, s[0], high), jnp.where(here, s[1], low)
        packed.append((high, low))
    line = jnp.zeros(BLK, F32)
    for n, s in enumerate(packed):
        for shift in (64, 32, 16, 8, 4, 2, 1):
            s = pair_add(s, tuple(pltpu.roll(v, shift, 1) for v in s))
        away = iota(BLK, 1) - iota(BLK, 0) - 8 * n
        line = line + jnp.where(away == 0, s[0], F32(0)) + jnp.where(away == 64, s[1], F32(0))
    line = jnp.sum(line, axis=0, keepdims=True)
    out[...] = jnp.broadcast_to(line, out.shape)


def gathered(parts, pairs):
    lines = []
    for n in range(parts.shape[0] // 8):
        high = parts[8 * n : 8 * n + 8, :]
        lines.append((high, pltpu.roll(high, 64, 1)))
    s = total(lines)
    for shift in (4, 2, 1):
        s = pair_add(s, tuple(pltpu.roll(v, shift, 0) for v in s))
    entries, at = {}, 0

    def lane(k):
        return tuple(jnp.broadcast_to(v[:, k : k + 1], BLK) for v in s)

    zero = (jnp.zeros(BLK, F32), jnp.zeros(BLK, F32))
    for i, j in pairs:
        re, at = lane(at), at + 1
        im = zero
        if i != j:
            im, at = lane(at), at + 1
        entries[i, j] = (re, im)
        entries[j, i] = (re, negate(im)) if i != j else (re, im)
    return entries


def rows(v):
    return tuple(jnp.concatenate([x] * (ROWS // 8), axis=0) for x in v)


def scaled(v, re, im):
    return v[0] * re - v[1] * im, v[0] * im + v[1] * re


PAIRS_1 = ((1, 1), (2, 2), (0, 1), (1, 2), (0, 2))
PAIRS_2 = ((1, 1), (2, 2), (3, 3), (4, 4), (0, 1), (0, 2), (1, 2), (0, 3), (0, 4), (1, 3), (1, 4), (2, 3), (2, 4), (3, 4))


def scatter_source(me, n_slabs, weights, slab_of, cell_of, comp_of, source):
    upper = (iota((LANES, LANES), 0) <= iota((LANES, LANES), 1)).astype(jnp.bfloat16)
    key = (comp_of[...] * 8192 + cell_of[...]).astype(F32)
    n_blocks = key.shape[0]
    slots = n_blocks * CAP

    @pl.loop(0, len(SLABS))
    def _(s):
        slab = lax.rem(me + s + SLABS[0] + n_slabs, n_slabs)
        mine = slab_of[...] == slab
        mine_f = jnp.where(mine, F32(1), F32(0))
        rank = jnp.dot(mine_f.astype(jnp.bfloat16), upper, preferred_element_type=F32)
        rank = jnp.where(mine, rank, F32(0))
        slot = (iota((n_blocks, CAP, LANES), 1) + 1).astype(F32)
        chosen = rank[:, None, :] == slot

        def column(values):
            v = jnp.where(chosen, values[:, None, :], F32(0))
            return jnp.sum(v, axis=2, keepdims=True).reshape(slots, 1)

        place = column(key).astype(jnp.int32)
        hot_z = (place & (LANES - 1)) == iota((slots, LANES), 1)
        hot_row = jnp.where((place >> 7) == iota((slots, 256), 1), F32(1), F32(0))
        put = jnp.concatenate(
            [jnp.where(hot_z, column(weights[:, part, :]), F32(0)) for part in range(2)], axis=1
        )
        grid = lax.dot_general(
            hot_row,
            put,
            (((0,), (0,)), ((), ())),
            precision=lax.Precision.HIGHEST,
            preferred_element_type=F32,
        )
        for part in range(2):
            for comp in range(3):
                for plane in range(2):
                    row = comp * 64 + plane * 32
                    source[3 * part + comp, 2 * s + plane] = grid[
                        row : row + 32, part * LANES : (part + 1) * LANES
                    ]


def start_kernel(
    n_slabs, own, b2, b1, a1, a2, a3, weights, slab_of, cell_of, comp_of, freqs, pair,
    p0_out, p1_out, p2_out, damp_out, gram_out,
    field, damping, source, p0, p1,
):
    me = lax.axis_index("space")
    wave = freqs[pair[0]]
    for s, ref in enumerate((b2, b1, own, a1, a2, a3)):
        for k in range(6):
            field[k, 2 * s : 2 * s + 2] = ref[2 * k : 2 * k + 2]
        damping[2 * s : 2 * s + 2] = ref[12:14] * wave
    scatter_source(me, n_slabs, weights, slab_of, cell_of, comp_of, source)

    def keep_p0(part, comp, at, value):
        p0[3 * part + comp, at] = source[3 * part + comp, at] - value

    def keep_p1(part, comp, at, value):
        p1[3 * part + comp, at] = value

    def keep_p2(part, comp, at, value):
        p2_out[3 * part + comp, at - 3] = value

    apply(me, field, damping, -4, 1, 11, keep_p0)
    apply(me, p0, damping, -4, 2, 10, keep_p1)
    apply(me, p1, damping, -4, 3, 9, keep_p2)
    for k in range(6):
        p0_out[k] = p0[k, 3:9]
        p1_out[k] = p1[k, 3:9]
    damp_out[...] = damping[3:9]
    gram(((p0, 5), (p1, 5), (p2_out, 2)), PAIRS_1, gram_out)


def middle_kernel(
    parts, p0, p1, p2, damping, own,
    xs_out, r_out, d_out, m_out, f_out, gram_out,
    r, m, f, g, h,
):
    me = lax.axis_index("space")
    e = gathered(parts, PAIRS_1)
    den = e[1, 1][0][0]
    a = over(e[1, 0], den)
    t = csum([e[1, 1], mix(e[1, 2], cneg(a))])
    b = cneg(over(t, den))
    u = (F32(1) + b[0], b[1])
    w = [conj(csum([mix(e[i, 1], u), mix(e[i, 2], cneg(a))])) for i in range(3)]
    num = csum([w[0], mix(w[1], cneg(a))])
    den = pair_add(mix_re(w[1], u), mix_re(w[2], cneg(a)))[0]
    step = over(num, den)
    su = cmul(step, u)
    s = (a[0] + su[0], a[1] + su[1])
    v = cmul(step, a)
    a, u, s, v = rows(a), rows(u), rows(s), rows(v)

    @pl.loop(0, 6)
    def _(at):
        for c in range(3):
            v0 = (p0[c, at], p0[3 + c, at])
            v1 = (p1[c, at], p1[3 + c, at])
            v2 = (p2[c, at], p2[3 + c, at])
            s1, w2 = scaled(s, *v1), scaled(v, *v2)
            u1, a2 = scaled(u, *v1), scaled(a, *v2)
            for part in range(2):
                r[3 * part + c, at] = (v0[part] - s1[part]) + w2[part]
                m[3 * part + c, at] = u1[part] - a2[part]

    for plane in range(2):
        for c in range(3):
            v0 = (p0[c, 1 + plane], p0[3 + c, 1 + plane])
            v1 = (p1[c, 1 + plane], p1[3 + c, 1 + plane])
            s0, w1 = scaled(s, *v0), scaled(v, *v1)
            u0, a1 = scaled(u, *v0), scaled(a, *v1)
            for part in range(2):
                k = 2 * (3 * part + c) + plane
                xs_out[k] = (own[k] + s0[part]) - w1[part]
                d_out[k] = u0[part] - a1[part]
                r_out[k] = r[3 * part + c, 1 + plane]
                m_out[k] = m[3 * part + c, 1 + plane]

    def into(ref):
        def store(part, comp, at, value):
            ref[3 * part + comp, at] = value

        return store

    apply(me, r, damping, -1, 1, 5, into(f))
    apply(me, m, damping, -1, 2, 4, into(g))
    apply(me, f, damping, -1, 2, 4, into(h))
    for k in range(6):
        f_out[2 * k : 2 * k + 2] = f[k, 1:3]
    gram(((r, 2), (m, 2), (f, 2), (g, 2), (h, 2)), PAIRS_2, gram_out)


def end_kernel(parts, xs, r, d, m, f, background, freqs, pair, adjoint_out, terms_out):
    wave = freqs[pair[0]]
    e = gathered(parts, PAIRS_2)
    b = cneg(over(e[1, 2], e[1, 1][0][0]))
    w = [conj(csum([mix(e[i, 1], b), e[i, 2]])) for i in range(5)]
    den = pair_add(mix_re(w[1], b), w[2][0])[0]
    a = over(w[0], den)
    ab = cmul(a, b)
    t = csum([w[2], mix(w[3], cneg(ab)), mix(w[4], cneg(a))])
    b2 = cneg(over(t, den))
    q1, q2 = (F32(1) + b2[0], b2[1]), cmul(b2, b)
    mapped = (q2, q1, cneg(ab), cneg(a))
    w = [conj(csum([mix(e[i, 1 + k], q) for k, q in enumerate(mapped)])) for i in range(5)]
    num = csum([w[0], mix(w[1], cneg(ab)), mix(w[2], cneg(a))])
    den = total([mix_re(w[1 + k], q) for k, q in enumerate(mapped)])[0]
    a2 = over(num, den)
    to_r, to_d = cmul(a2, q1), cmul(a2, q2)
    to_r = rows((a[0] + to_r[0], a[1] + to_r[1]))
    to_d = rows((ab[0] + to_d[0], ab[1] + to_d[1]))
    to_f, to_m = rows(cmul(a2, a)), rows(cmul(a2, ab))
    for plane in range(2):
        terms = jnp.zeros((ROWS, LANES), F32)
        for c in range(3):
            k, q = 2 * c + plane, 2 * (3 + c) + plane
            add = [
                scaled(to_r, r[k], r[q]),
                scaled(to_d, d[k], d[q]),
                cneg(scaled(to_f, f[k], f[q])),
                cneg(scaled(to_m, m[k], m[q])),
            ]
            re = xs[k] + ((add[0][0] + add[1][0]) + (add[2][0] + add[3][0]))
            im = xs[q] + ((add[0][1] + add[1][1]) + (add[2][1] + add[3][1]))
            adjoint_out[k] = re
            adjoint_out[q] = im
            terms = terms + (re * background[q] + im * background[k])
        terms = terms * wave
        n_src = terms_out.shape[0]
        part = ROWS // n_src
        for n in range(n_src):
            terms_out[n, plane * part : (plane + 1) * part] = terms[n * part : (n + 1) * part]


def shaped(*shape):
    return jax.ShapeDtypeStruct(shape, F32)


def kernel(body, name, in_specs, outs, scratch, flops):
    return pl.pallas_call(
        body,
        name=name,
        in_specs=in_specs,
        out_specs=tuple(spec() for _ in outs),
        out_shape=tuple(outs),
        scratch_shapes=[pltpu.VMEM(s, F32) for s in scratch],
        compiler_params=pltpu.CompilerParams(vmem_limit_bytes=VMEM_BYTES),
        cost_estimate=pl.CostEstimate(flops=flops, bytes_accessed=3_000_000, transcendentals=0),
    )


def shards(
    background,
    warm_start,
    conductivity,
    frequencies,
    pair_freq,
    weighted_residual,
    datum_layer_index,
    receiver_flat_cell,
    receiver_component,
):
    n_slabs, n_src = lax.axis_size("space"), lax.axis_size("src")
    own = warm_start.reshape(12, ROWS, LANES)
    message = jnp.concatenate([own, conductivity], axis=0)

    def from_slab(away):
        route = [((i + away) % n_slabs, i) for i in range(n_slabs)]
        return lax.ppermute(message, "space", route)

    window = [from_slab(away) for away in (-2, -1, 1, 2, 3)]
    weights = jnp.broadcast_to(weighted_residual.reshape(1, 2, LANES), (n_slabs, 2, LANES))
    weights = lax.all_to_all(weights, "space", split_axis=0, concat_axis=0, tiled=True)
    plane = (ROWS, LANES)
    slab_of = datum_layer_index.reshape(n_slabs, LANES)
    cell_of = receiver_flat_cell.reshape(n_slabs, LANES)
    comp_of = receiver_component.reshape(n_slabs, LANES)
    smem = spec(pltpu.SMEM)
    six = shaped(6, 6, *plane)
    p0, p1, p2, damping, parts = kernel(
        functools.partial(start_kernel, n_slabs),
        "start",
        [spec()] * 10 + [smem] * 2,
        [six, six, six, shaped(6, *plane), shaped(n_slabs, LANES)],
        [(6, 12, *plane), (12, *plane), (6, 12, *plane), (6, 12, *plane), (6, 12, *plane)],
        60_000_000,
    )(message, *window, weights, slab_of, cell_of, comp_of, frequencies, pair_freq)
    parts = lax.all_to_all(parts, "space", split_axis=0, concat_axis=0, tiled=True)
    two = shaped(12, *plane)
    xs, r, d, m, f, parts = kernel(
        middle_kernel,
        "middle",
        [spec()] * 6,
        [two] * 5 + [shaped(n_slabs, LANES)],
        [(6, 6, *plane)] * 5,
        40_000_000,
    )(parts, p0, p1, p2, damping, own)
    parts = lax.all_to_all(parts, "space", split_axis=0, concat_axis=0, tiled=True)
    adjoint, terms = kernel(
        end_kernel,
        "end",
        [spec()] * 7 + [smem] * 2,
        [two, shaped(n_src, 2 * (ROWS // n_src), LANES)],
        [],
        5_000_000,
    )(parts, xs, r, d, m, f, background.reshape(12, *plane), frequencies, pair_freq)
    terms = lax.all_to_all(terms, "src", split_axis=0, concat_axis=0, tiled=True)
    gradient = jnp.sum(terms, axis=0).reshape(2, ROWS // n_src, LANES)
    return adjoint.reshape(warm_start.shape), gradient


def solution(mesh):
    placed = (
        P(None, "src", None, "space", None, None),
        P(None, "src", None, "space", None, None),
        P("space", None, None),
        P(),
        P("src"),
        P(None, "src", "space"),
        P(),
        P(),
        P(),
    )
    return jax.shard_map(
        shards,
        mesh=mesh,
        in_specs=placed,
        out_specs=(P(None, "src", None, "space", None, None), P("space", "src", None)),
        check_vma=False,
    )
```

```python
import functools

import jax
import jax.numpy as jnp
from jax import lax
from jax.experimental import pallas as pl
from jax.experimental.pallas import tpu as pltpu
from jax.sharding import PartitionSpec as P

F32 = jnp.float32
SLABS = (-2, -1, 0, 1, 2, 3)
ROWS, LANES = 32, 128
BLK = (8, 128)
CAP = 8
VMEM_BYTES = 14 * 1024 * 1024


def spec(space=pltpu.VMEM):
    return pl.BlockSpec(memory_space=space)


def iota(shape, axis):
    return lax.broadcasted_iota(jnp.int32, shape, axis)


def two_sum(a, b):
    s = a + b
    t = s - a
    return s, (a - (s - t)) + (b - t)


def split(a):
    t = a * F32(4097.0)
    high = t - (t - a)
    return high, a - high


def product_error(p, a, b):
    (ah, al), (bh, bl) = a, b
    return ((ah * bh - p) + ah * bl + al * bh) + al * bl


def pair_add(a, b):
    s, e = two_sum(a[0], b[0])
    e = e + (a[1] + b[1])
    h = s + e
    return h, e - (h - s)


def pair_scale(a, c):
    p = a[0] * c
    e = product_error(p, split(a[0]), split(c)) + a[1] * c
    h = p + e
    return h, e - (h - p)


def negate(a):
    return tuple(-v for v in a)


def total(terms):
    return functools.reduce(pair_add, terms)


def mix_re(g, v):
    return pair_add(pair_scale(g[0], v[0]), negate(pair_scale(g[1], v[1])))


def mix(g, v):
    return mix_re(g, v), pair_add(pair_scale(g[0], v[1]), pair_scale(g[1], v[0]))


def csum(terms):
    return total([t[0] for t in terms]), total([t[1] for t in terms])


def conj(g):
    return g[0], negate(g[1])


def cneg(v):
    return -v[0], -v[1]


def cmul(a, b):
    return a[0] * b[0] - a[1] * b[1], a[0] * b[1] + a[1] * b[0]


def over(g, den):
    return g[0][0] / den, g[1][0] / den


def y_next(e):
    return jnp.where(iota(e.shape, 0) == ROWS - 1, F32(0), pltpu.roll(e, ROWS - 1, 0))


def z_next(e):
    return jnp.where(iota(e.shape, 1) == LANES - 1, F32(0), pltpu.roll(e, LANES - 1, 1))


def y_prev(h, first):
    return jnp.where(iota(h.shape, 0) == 0, first, pltpu.roll(h, 1, 0))


def z_prev(h, first):
    return jnp.where(iota(h.shape, 1) == 0, first, pltpu.roll(h, 1, 1))


def forward_yz(ex, ey, ez, ey_up, ez_up):
    hy = (z_next(ex) - ex) - (ez_up - ez)
    hz = (ey_up - ey) - (y_next(ex) - ex)
    return hy, hz


def curl_curl(field, part, at, above, below, before):
    ex, ey, ez = (field[3 * part + c, at] for c in range(3))
    ey_up, ez_up = (field[3 * part + c, at + 1] * above for c in (1, 2))
    hx = (y_next(ez) - ez) - (z_next(ey) - ey)
    hy, hz = forward_yz(ex, ey, ez, ey_up, ez_up)
    edge = F32(1) - below
    hy_dn = before[0] * below - ez * edge
    hz_dn = before[1] * below + ey * edge
    result = (
        (hz - y_prev(hz, -ex)) - (hy - z_prev(hy, ex)),
        (hx - z_prev(hx, -ey)) - (hz - hz_dn),
        (hy - hy_dn) - (hx - y_prev(hx, ez)),
    )
    return result, (hy, hz)


def apply(me, field, damping, first, low, high, store):
    def plane(at, before):
        grid_plane = lax.rem(2 * me + first + at + 64, 64)
        above = jnp.where(grid_plane == 63, F32(0), F32(1))
        below = jnp.where(grid_plane == 0, F32(0), F32(1))
        damp = damping[at]
        real, real_h = curl_curl(field, 0, at, above, below, before[:2])
        for c in range(3):
            store(0, c, at, real[c] - damp * field[3 + c, at])
        imag, imag_h = curl_curl(field, 1, at, above, below, before[2:])
        for c in range(3):
            store(1, c, at, imag[c] + damp * field[c, at])
        return real_h + imag_h

    below_first = []
    for part in range(2):
        under = [field[3 * part + c, low - 1] for c in range(3)]
        below_first += forward_yz(*under, *(field[3 * part + c, low] for c in (1, 2)))
    lax.fori_loop(low, high, plane, tuple(below_first))


def gram(fields, pairs, out, size=4):
    names = sorted({k for pair in pairs for k in pair})

    def block(step, k, part):
        comp, rest = step // 8, lax.rem(step, 8)
        plane, row = rest // 4, pl.multiple_of(lax.rem(rest, 4) * 8, 8)
        ref, start = fields[k]
        return ref[3 * part + comp, start + plane, pl.ds(row, 8), :]

    def peak(step, tops):
        return tuple(
            jnp.maximum(top, jnp.maximum(jnp.abs(block(step, k, 0)), jnp.abs(block(step, k, 1))))
            for k, top in zip(names, tops)
        )

    zero = jnp.zeros(BLK, F32)
    tops = lax.fori_loop(0, 24, peak, tuple(zero for _ in names), unroll=2)
    grids = {k: top * F32(2.0**15) for k, top in zip(names, tops)}
    sums = []
    for first in range(0, len(pairs), size):
        group = pairs[first : first + size]
        used = sorted({k for pair in group for k in pair})
        count = sum(1 if i == j else 2 for i, j in group)

        def body(step, acc, group=group, used=used):
            values = {}
            for k in used:
                for part in range(2):
                    v = block(step, k, part)
                    high = (v + grids[k]) - grids[k]
                    values[k, part] = v, high, v - high

            def products(a, b):
                return a[1] * b[1], a[1] * b[2] + a[2] * b[0]

            new = []
            for i, j in group:
                x, y = products(values[i, 0], values[j, 0]), products(values[i, 1], values[j, 1])
                re = acc[len(new)]
                new.append(tuple(re[n] + (x[n] + y[n]) for n in range(2)))
                if i != j:
                    x, y = products(values[i, 0], values[j, 1]), products(values[i, 1], values[j, 0])
                    im = acc[len(new)]
                    new.append(tuple(im[n] + (x[n] - y[n]) for n in range(2)))
            return tuple(new)

        sums += list(
            lax.fori_loop(0, 24, body, tuple((zero, zero) for _ in range(count)), unroll=2)
        )
    packed = []
    for first in range(0, len(sums), 8):
        high = low = jnp.zeros(BLK, F32)
        for k, s in enumerate(sums[first : first + 8]):
            for shift in (4, 2, 1):
                s = pair_add(s, tuple(pltpu.roll(v, shift, 0) for v in s))
            here = iota(BLK, 0) == k
            high, low = jnp.where(here, s[0], high), jnp.where(here, s[1], low)
        packed.append((high, low))
    line = jnp.zeros(BLK, F32)
    for n, s in enumerate(packed):
        for shift in (64, 32, 16, 8, 4, 2, 1):
            s = pair_add(s, tuple(pltpu.roll(v, shift, 1) for v in s))
        away = iota(BLK, 1) - iota(BLK, 0) - 8 * n
        line = line + jnp.where(away == 0, s[0], F32(0)) + jnp.where(away == 64, s[1], F32(0))
    line = jnp.sum(line, axis=0, keepdims=True)
    out[...] = jnp.broadcast_to(line, out.shape)


def gathered(parts, pairs):
    lines = []
    for n in range(parts.shape[0] // 8):
        high = parts[8 * n : 8 * n + 8, :]
        lines.append((high, pltpu.roll(high, 64, 1)))
    s = total(lines)
    for shift in (4, 2, 1):
        s = pair_add(s, tuple(pltpu.roll(v, shift, 0) for v in s))
    entries, at = {}, 0

    def lane(k):
        return tuple(jnp.broadcast_to(v[:, k : k + 1], BLK) for v in s)

    zero = (jnp.zeros(BLK, F32), jnp.zeros(BLK, F32))
    for i, j in pairs:
        re, at = lane(at), at + 1
        im = zero
        if i != j:
            im, at = lane(at), at + 1
        entries[i, j] = (re, im)
        entries[j, i] = (re, negate(im)) if i != j else (re, im)
    return entries


def rows(v):
    return tuple(jnp.concatenate([x] * (ROWS // 8), axis=0) for x in v)


def scaled(v, re, im):
    return v[0] * re - v[1] * im, v[0] * im + v[1] * re


PAIRS_1 = ((1, 1), (2, 2), (0, 1), (1, 2), (0, 2))
PAIRS_2 = ((1, 1), (2, 2), (3, 3), (4, 4), (0, 1), (0, 2), (1, 2), (0, 3), (0, 4), (1, 3), (1, 4), (2, 3), (2, 4), (3, 4))


def place_measurements(me, n_slabs, slab_of, cell_of, comp_of, ranks, hot_z, hot_row):
    upper = (iota((LANES, LANES), 0) <= iota((LANES, LANES), 1)).astype(jnp.bfloat16)
    key = (comp_of[...] * 8192 + cell_of[...]).astype(F32)
    n_blocks = key.shape[0]
    slots = n_blocks * CAP
    same = (iota((slots, slots), 0) == iota((slots, slots), 1)).astype(jnp.bfloat16)

    @pl.loop(0, len(SLABS))
    def _(s):
        slab = lax.rem(me + s + SLABS[0] + n_slabs, n_slabs)
        mine = slab_of[...] == slab
        mine_f = jnp.where(mine, F32(1), F32(0))
        rank = jnp.dot(mine_f.astype(jnp.bfloat16), upper, preferred_element_type=F32)
        rank = jnp.where(mine, rank, F32(0))
        ranks[s] = rank
        place = column(rank, key).astype(jnp.int32)
        at_z = (place & (LANES - 1)) == iota((slots, LANES), 1)
        hot_z[s] = jnp.where(at_z, F32(1), F32(0))
        at_row = jnp.where((place >> 7) == iota((slots, 256), 1), F32(1), F32(0))
        turned = lax.dot_general(
            at_row.astype(jnp.bfloat16), same, (((0,), (0,)), ((), ())), preferred_element_type=F32
        )
        hot_row[s] = turned.astype(jnp.bfloat16)


def column(rank, values):
    n_blocks = rank.shape[0]
    slot = (iota((n_blocks, CAP, LANES), 1) + 1).astype(F32)
    v = jnp.where(rank[:, None, :] == slot, values[:, None, :], F32(0))
    return jnp.sum(v, axis=2, keepdims=True).reshape(n_blocks * CAP, 1)


def scatter_source(weights, ranks, hot_z, hot_row, source):
    @pl.loop(0, len(SLABS))
    def _(s):
        put = jnp.concatenate(
            [hot_z[s] * column(ranks[s], weights[:, part, :]) for part in range(2)], axis=1
        )
        grid = None
        for _ in range(3):
            piece = put.astype(jnp.bfloat16)
            put = put - piece.astype(F32)
            term = jnp.dot(hot_row[s], piece, preferred_element_type=F32)
            grid = term if grid is None else grid + term
        for part in range(2):
            for comp in range(3):
                for plane in range(2):
                    row = comp * 64 + plane * 32
                    source[3 * part + comp, 2 * s + plane] = grid[
                        row : row + 32, part * LANES : (part + 1) * LANES
                    ]


def into(ref):
    def store(part, comp, at, value):
        ref[3 * part + comp, at] = value

    return store


def place_kernel(
    n_slabs, slab_of, cell_of, comp_of, freqs, pair, ranks, hot_z, hot_row, wave
):
    me = lax.axis_index("space")
    wave[...] = jnp.full(BLK, freqs[pair[0]], F32)
    place_measurements(me, n_slabs, slab_of, cell_of, comp_of, ranks, hot_z, hot_row)


def start_kernel(
    own, b2, b1, a1, a2, a3, weights, ranks, hot_z, hot_row, wave,
    p0_out, p1_out, p2_out, damp_out, gram_out,
    field, damping, source, p0, p1,
):
    me = lax.axis_index("space")
    for s, ref in enumerate((b2, b1, own, a1, a2, a3)):
        for k in range(6):
            field[k, 2 * s : 2 * s + 2] = ref[2 * k : 2 * k + 2]
        damping[2 * s : 2 * s + 2] = ref[12:14] * wave[0:1, :]
    scatter_source(weights, ranks, hot_z, hot_row, source)

    def keep_p0(part, comp, at, value):
        p0[3 * part + comp, at] = source[3 * part + comp, at] - value

    def keep_p2(part, comp, at, value):
        p2_out[3 * part + comp, at - 3] = value

    apply(me, field, damping, -4, 1, 11, keep_p0)
    apply(me, p0, damping, -4, 2, 10, into(p1))
    apply(me, p1, damping, -4, 3, 9, keep_p2)
    for k in range(6):
        p0_out[k] = p0[k, 3:9]
        p1_out[k] = p1[k, 3:9]
    damp_out[...] = damping[3:9]
    gram(((p0, 5), (p1, 5), (p2_out, 2)), PAIRS_1, gram_out)


def middle_kernel(
    parts, p0, p1, p2, damping, own,
    xs_out, r_out, d_out, m_out, f_out, gram_out,
    r, m, f, g, h,
):
    me = lax.axis_index("space")
    e = gathered(parts, PAIRS_1)
    den = e[1, 1][0][0]
    a = over(e[1, 0], den)
    t = csum([e[1, 1], mix(e[1, 2], cneg(a))])
    b = cneg(over(t, den))
    u = (F32(1) + b[0], b[1])
    w = [conj(csum([mix(e[i, 1], u), mix(e[i, 2], cneg(a))])) for i in range(3)]
    num = csum([w[0], mix(w[1], cneg(a))])
    den = pair_add(mix_re(w[1], u), mix_re(w[2], cneg(a)))[0]
    step = over(num, den)
    su = cmul(step, u)
    s = (a[0] + su[0], a[1] + su[1])
    v = cmul(step, a)
    a, u, s, v = rows(a), rows(u), rows(s), rows(v)

    @pl.loop(0, 6)
    def _(at):
        for c in range(3):
            v0 = (p0[c, at], p0[3 + c, at])
            v1 = (p1[c, at], p1[3 + c, at])
            v2 = (p2[c, at], p2[3 + c, at])
            s1, w2 = scaled(s, *v1), scaled(v, *v2)
            u1, a2 = scaled(u, *v1), scaled(a, *v2)
            for part in range(2):
                r[3 * part + c, at] = (v0[part] - s1[part]) + w2[part]
                m[3 * part + c, at] = u1[part] - a2[part]

    for plane in range(2):
        for c in range(3):
            v0 = (p0[c, 1 + plane], p0[3 + c, 1 + plane])
            v1 = (p1[c, 1 + plane], p1[3 + c, 1 + plane])
            s0, w1 = scaled(s, *v0), scaled(v, *v1)
            u0, a1 = scaled(u, *v0), scaled(a, *v1)
            for part in range(2):
                k = 2 * (3 * part + c) + plane
                xs_out[k] = (own[k] + s0[part]) - w1[part]
                d_out[k] = u0[part] - a1[part]
                r_out[k] = r[3 * part + c, 1 + plane]
                m_out[k] = m[3 * part + c, 1 + plane]

    apply(me, r, damping, -1, 1, 5, into(f))
    apply(me, m, damping, -1, 2, 4, into(g))
    apply(me, f, damping, -1, 2, 4, into(h))
    for k in range(6):
        f_out[2 * k : 2 * k + 2] = f[k, 1:3]
    gram(((r, 2), (m, 2), (f, 2), (g, 2), (h, 2)), PAIRS_2, gram_out)


def end_kernel(parts, xs, r, d, m, f, background, wave, adjoint_out, terms_out):
    e = gathered(parts, PAIRS_2)
    b = cneg(over(e[1, 2], e[1, 1][0][0]))
    w = [conj(csum([mix(e[i, 1], b), e[i, 2]])) for i in range(5)]
    den = pair_add(mix_re(w[1], b), w[2][0])[0]
    a = over(w[0], den)
    ab = cmul(a, b)
    t = csum([w[2], mix(w[3], cneg(ab)), mix(w[4], cneg(a))])
    b2 = cneg(over(t, den))
    q1, q2 = (F32(1) + b2[0], b2[1]), cmul(b2, b)
    mapped = (q2, q1, cneg(ab), cneg(a))
    w = [conj(csum([mix(e[i, 1 + k], q) for k, q in enumerate(mapped)])) for i in range(5)]
    num = csum([w[0], mix(w[1], cneg(ab)), mix(w[2], cneg(a))])
    den = total([mix_re(w[1 + k], q) for k, q in enumerate(mapped)])[0]
    a2 = over(num, den)
    to_r, to_d = cmul(a2, q1), cmul(a2, q2)
    to_r = rows((a[0] + to_r[0], a[1] + to_r[1]))
    to_d = rows((ab[0] + to_d[0], ab[1] + to_d[1]))
    to_f, to_m = rows(cmul(a2, a)), rows(cmul(a2, ab))
    for plane in range(2):
        terms = jnp.zeros((ROWS, LANES), F32)
        for c in range(3):
            k, q = 2 * c + plane, 2 * (3 + c) + plane
            add = [
                scaled(to_r, r[k], r[q]),
                scaled(to_d, d[k], d[q]),
                cneg(scaled(to_f, f[k], f[q])),
                cneg(scaled(to_m, m[k], m[q])),
            ]
            re = xs[k] + ((add[0][0] + add[1][0]) + (add[2][0] + add[3][0]))
            im = xs[q] + ((add[0][1] + add[1][1]) + (add[2][1] + add[3][1]))
            adjoint_out[k] = re
            adjoint_out[q] = im
            terms = terms + (re * background[q] + im * background[k])
        terms = terms * wave[0:1, :]
        n_src = terms_out.shape[0]
        part = ROWS // n_src
        for n in range(n_src):
            terms_out[n, plane * part : (plane + 1) * part] = terms[n * part : (n + 1) * part]


def shaped(*shape):
    return jax.ShapeDtypeStruct(shape, F32)


def kernel(body, name, in_specs, outs, scratch, flops):
    return pl.pallas_call(
        body,
        name=name,
        in_specs=in_specs,
        out_specs=tuple(spec() for _ in outs),
        out_shape=tuple(outs),
        scratch_shapes=[pltpu.VMEM(s, F32) for s in scratch],
        compiler_params=pltpu.CompilerParams(vmem_limit_bytes=VMEM_BYTES),
        cost_estimate=pl.CostEstimate(flops=flops, bytes_accessed=3_000_000, transcendentals=0),
    )


def shards(
    background,
    warm_start,
    conductivity,
    frequencies,
    pair_freq,
    weighted_residual,
    datum_layer_index,
    receiver_flat_cell,
    receiver_component,
):
    n_slabs, n_src = lax.axis_size("space"), lax.axis_size("src")
    own = warm_start.reshape(12, ROWS, LANES)
    message = jnp.concatenate([own, conductivity], axis=0)

    def from_slab(away):
        route = [((i + away) % n_slabs, i) for i in range(n_slabs)]
        return lax.ppermute(message, "space", route)

    window = [from_slab(away) for away in (-2, -1, 1, 2, 3)]
    weights = jnp.broadcast_to(weighted_residual.reshape(1, 2, LANES), (n_slabs, 2, LANES))
    weights = lax.all_to_all(weights, "space", split_axis=0, concat_axis=0, tiled=True)
    plane = (ROWS, LANES)
    slab_of = datum_layer_index.reshape(n_slabs, LANES)
    cell_of = receiver_flat_cell.reshape(n_slabs, LANES)
    comp_of = receiver_component.reshape(n_slabs, LANES)
    smem = spec(pltpu.SMEM)
    six = shaped(6, 6, *plane)
    slots = n_slabs * CAP
    places = kernel(
        functools.partial(place_kernel, n_slabs),
        "place",
        [spec()] * 3 + [smem] * 2,
        [
            shaped(len(SLABS), *plane),
            shaped(len(SLABS), slots, LANES),
            jax.ShapeDtypeStruct((len(SLABS), 256, slots), jnp.bfloat16),
            shaped(*BLK),
        ],
        [],
        20_000_000,
    )(slab_of, cell_of, comp_of, frequencies, pair_freq)
    wave = places[-1]
    p0, p1, p2, damping, parts = kernel(
        start_kernel,
        "start",
        [spec()] * 11,
        [six, six, six, shaped(6, *plane), shaped(n_slabs, LANES)],
        [(6, 12, *plane), (12, *plane), (6, 12, *plane), (6, 12, *plane), (6, 12, *plane)],
        40_000_000,
    )(message, *window, weights, *places)
    parts = lax.all_to_all(parts, "space", split_axis=0, concat_axis=0, tiled=True)
    two = shaped(12, *plane)
    xs, r, d, m, f, parts = kernel(
        middle_kernel,
        "middle",
        [spec()] * 6,
        [two] * 5 + [shaped(n_slabs, LANES)],
        [(6, 6, *plane)] * 5,
        40_000_000,
    )(parts, p0, p1, p2, damping, own)
    parts = lax.all_to_all(parts, "space", split_axis=0, concat_axis=0, tiled=True)
    adjoint, terms = kernel(
        end_kernel,
        "end",
        [spec()] * 8,
        [two, shaped(n_src, 2 * (ROWS // n_src), LANES)],
        [],
        5_000_000,
    )(parts, xs, r, d, m, f, background.reshape(12, *plane), wave)
    terms = lax.all_to_all(terms, "src", split_axis=0, concat_axis=0, tiled=True)
    gradient = jnp.sum(terms, axis=0).reshape(2, ROWS // n_src, LANES)
    return adjoint.reshape(warm_start.shape), gradient


def solution(mesh):
    placed = (
        P(None, "src", None, "space", None, None),
        P(None, "src", None, "space", None, None),
        P("space", None, None),
        P(),
        P("src"),
        P(None, "src", "space"),
        P(),
        P(),
        P(),
    )
    return jax.shard_map(
        shards,
        mesh=mesh,
        in_specs=placed,
        out_specs=(P(None, "src", None, "space", None, None), P("space", "src", None)),
        check_vma=False,
    )
```

```python
import functools

import jax
import jax.numpy as jnp
from jax import lax
from jax.experimental import pallas as pl
from jax.experimental.pallas import tpu as pltpu
from jax.sharding import PartitionSpec as P

F32 = jnp.float32
SLABS = (-2, -1, 0, 1, 2, 3)
ROWS, LANES = 32, 128
BLK = (8, 128)
CAP = 8
VMEM_BYTES = 14 * 1024 * 1024


def spec(space=pltpu.VMEM):
    return pl.BlockSpec(memory_space=space)


def iota(shape, axis):
    return lax.broadcasted_iota(jnp.int32, shape, axis)


def two_sum(a, b):
    s = a + b
    t = s - a
    return s, (a - (s - t)) + (b - t)


def split(a):
    t = a * F32(4097.0)
    high = t - (t - a)
    return high, a - high


def product_error(p, a, b):
    (ah, al), (bh, bl) = a, b
    return ((ah * bh - p) + ah * bl + al * bh) + al * bl


def pair_add(a, b):
    s, e = two_sum(a[0], b[0])
    e = e + (a[1] + b[1])
    h = s + e
    return h, e - (h - s)


def pair_scale(a, c):
    p = a[0] * c
    e = product_error(p, split(a[0]), split(c)) + a[1] * c
    h = p + e
    return h, e - (h - p)


def negate(a):
    return tuple(-v for v in a)


def total(terms):
    return functools.reduce(pair_add, terms)


def mix_re(g, v):
    return pair_add(pair_scale(g[0], v[0]), negate(pair_scale(g[1], v[1])))


def mix(g, v):
    return mix_re(g, v), pair_add(pair_scale(g[0], v[1]), pair_scale(g[1], v[0]))


def csum(terms):
    return total([t[0] for t in terms]), total([t[1] for t in terms])


def conj(g):
    return g[0], negate(g[1])


def cneg(v):
    return -v[0], -v[1]


def cmul(a, b):
    return a[0] * b[0] - a[1] * b[1], a[0] * b[1] + a[1] * b[0]


def over(g, den):
    return g[0][0] / den, g[1][0] / den


def y_next(e):
    return jnp.where(iota(e.shape, 0) == ROWS - 1, F32(0), pltpu.roll(e, ROWS - 1, 0))


def z_next(e):
    return jnp.where(iota(e.shape, 1) == LANES - 1, F32(0), pltpu.roll(e, LANES - 1, 1))


def y_prev(h, first):
    return jnp.where(iota(h.shape, 0) == 0, first, pltpu.roll(h, 1, 0))


def z_prev(h, first):
    return jnp.where(iota(h.shape, 1) == 0, first, pltpu.roll(h, 1, 1))


def forward_yz(ex, ey, ez, ey_up, ez_up):
    hy = (z_next(ex) - ex) - (ez_up - ez)
    hz = (ey_up - ey) - (y_next(ex) - ex)
    return hy, hz


def curl_curl(field, part, at, above, below, before):
    ex, ey, ez = (field[3 * part + c, at] for c in range(3))
    ey_up, ez_up = (field[3 * part + c, at + 1] * above for c in (1, 2))
    hx = (y_next(ez) - ez) - (z_next(ey) - ey)
    hy, hz = forward_yz(ex, ey, ez, ey_up, ez_up)
    edge = F32(1) - below
    hy_dn = before[0] * below - ez * edge
    hz_dn = before[1] * below + ey * edge
    result = (
        (hz - y_prev(hz, -ex)) - (hy - z_prev(hy, ex)),
        (hx - z_prev(hx, -ey)) - (hz - hz_dn),
        (hy - hy_dn) - (hx - y_prev(hx, ez)),
    )
    return result, (hy, hz)


def apply(me, field, damping, first, low, high, store, unroll=2):
    def plane(at, before):
        grid_plane = lax.rem(2 * me + first + at + 64, 64)
        above = jnp.where(grid_plane == 63, F32(0), F32(1))
        below = jnp.where(grid_plane == 0, F32(0), F32(1))
        damp = damping[at]
        real, real_h = curl_curl(field, 0, at, above, below, before[:2])
        for c in range(3):
            store(0, c, at, real[c] - damp * field[3 + c, at])
        imag, imag_h = curl_curl(field, 1, at, above, below, before[2:])
        for c in range(3):
            store(1, c, at, imag[c] + damp * field[c, at])
        return real_h + imag_h

    below_first = []
    for part in range(2):
        under = [field[3 * part + c, low - 1] for c in range(3)]
        below_first += forward_yz(*under, *(field[3 * part + c, low] for c in (1, 2)))
    lax.fori_loop(low, high, plane, tuple(below_first), unroll=unroll)


def gram(fields, pairs, out, size=14):
    names = sorted({k for pair in pairs for k in pair})

    def block(step, k, part):
        comp, rest = step // 8, lax.rem(step, 8)
        plane, row = rest // 4, pl.multiple_of(lax.rem(rest, 4) * 8, 8)
        ref, start = fields[k]
        return ref[3 * part + comp, start + plane, pl.ds(row, 8), :]

    def peak(step, tops):
        return tuple(
            jnp.maximum(top, jnp.maximum(jnp.abs(block(step, k, 0)), jnp.abs(block(step, k, 1))))
            for k, top in zip(names, tops)
        )

    zero = jnp.zeros(BLK, F32)
    tops = lax.fori_loop(0, 24, peak, tuple(zero for _ in names), unroll=2)
    grids = {k: top * F32(2.0**15) for k, top in zip(names, tops)}
    sums = []
    for first in range(0, len(pairs), size):
        group = pairs[first : first + size]
        used = sorted({k for pair in group for k in pair})
        count = sum(1 if i == j else 2 for i, j in group)

        def body(step, acc, group=group, used=used):
            values = {}
            for k in used:
                for part in range(2):
                    v = block(step, k, part)
                    high = (v + grids[k]) - grids[k]
                    values[k, part] = v, high, v - high

            def products(a, b):
                return a[1] * b[1], a[1] * b[2] + a[2] * b[0]

            new = []
            for i, j in group:
                x, y = products(values[i, 0], values[j, 0]), products(values[i, 1], values[j, 1])
                re = acc[len(new)]
                new.append(tuple(re[n] + (x[n] + y[n]) for n in range(2)))
                if i != j:
                    x, y = products(values[i, 0], values[j, 1]), products(values[i, 1], values[j, 0])
                    im = acc[len(new)]
                    new.append(tuple(im[n] + (x[n] - y[n]) for n in range(2)))
            return tuple(new)

        sums += list(
            lax.fori_loop(0, 24, body, tuple((zero, zero) for _ in range(count)), unroll=4)
        )
    packed = []
    for first in range(0, len(sums), 8):
        high = low = jnp.zeros(BLK, F32)
        for k, s in enumerate(sums[first : first + 8]):
            for shift in (4, 2, 1):
                s = pair_add(s, tuple(pltpu.roll(v, shift, 0) for v in s))
            here = iota(BLK, 0) == k
            high, low = jnp.where(here, s[0], high), jnp.where(here, s[1], low)
        packed.append((high, low))
    line = jnp.zeros(BLK, F32)
    for n, s in enumerate(packed):
        for shift in (64, 32, 16, 8, 4, 2, 1):
            s = pair_add(s, tuple(pltpu.roll(v, shift, 1) for v in s))
        away = iota(BLK, 1) - iota(BLK, 0) - 8 * n
        line = line + jnp.where(away == 0, s[0], F32(0)) + jnp.where(away == 64, s[1], F32(0))
    line = jnp.sum(line, axis=0, keepdims=True)
    out[...] = jnp.broadcast_to(line, out.shape)


def gathered(parts, pairs):
    lines = []
    for n in range(parts.shape[0] // 8):
        high = parts[8 * n : 8 * n + 8, :]
        lines.append((high, pltpu.roll(high, 64, 1)))
    s = total(lines)
    for shift in (4, 2, 1):
        s = pair_add(s, tuple(pltpu.roll(v, shift, 0) for v in s))
    entries, at = {}, 0

    def lane(k):
        return tuple(jnp.broadcast_to(v[:, k : k + 1], BLK) for v in s)

    zero = (jnp.zeros(BLK, F32), jnp.zeros(BLK, F32))
    for i, j in pairs:
        re, at = lane(at), at + 1
        im = zero
        if i != j:
            im, at = lane(at), at + 1
        entries[i, j] = (re, im)
        entries[j, i] = (re, negate(im)) if i != j else (re, im)
    return entries


def rows(v):
    return tuple(jnp.concatenate([x] * (ROWS // 8), axis=0) for x in v)


def scaled(v, re, im):
    return v[0] * re - v[1] * im, v[0] * im + v[1] * re


PAIRS_1 = ((1, 1), (2, 2), (0, 1), (1, 2), (0, 2))
PAIRS_2 = ((1, 1), (2, 2), (3, 3), (4, 4), (0, 1), (0, 2), (1, 2), (0, 3), (0, 4), (1, 3), (1, 4), (2, 3), (2, 4), (3, 4))


def place_measurements(me, n_slabs, slab_of, cell_of, comp_of, ranks, hot_z, hot_row):
    upper = (iota((LANES, LANES), 0) <= iota((LANES, LANES), 1)).astype(jnp.bfloat16)
    key = (comp_of[...] * 8192 + cell_of[...]).astype(F32)
    n_blocks = key.shape[0]
    slots = n_blocks * CAP
    same = (iota((slots, slots), 0) == iota((slots, slots), 1)).astype(jnp.bfloat16)

    @pl.loop(0, len(SLABS))
    def _(s):
        slab = lax.rem(me + s + SLABS[0] + n_slabs, n_slabs)
        mine = slab_of[...] == slab
        mine_f = jnp.where(mine, F32(1), F32(0))
        rank = jnp.dot(mine_f.astype(jnp.bfloat16), upper, preferred_element_type=F32)
        rank = jnp.where(mine, rank, F32(0))
        ranks[s] = rank
        place = column(rank, key).astype(jnp.int32)
        at_z = (place & (LANES - 1)) == iota((slots, LANES), 1)
        hot_z[s] = jnp.where(at_z, F32(1), F32(0))
        at_row = jnp.where((place >> 7) == iota((slots, 256), 1), F32(1), F32(0))
        turned = lax.dot_general(
            at_row.astype(jnp.bfloat16), same, (((0,), (0,)), ((), ())), preferred_element_type=F32
        )
        hot_row[s] = turned.astype(jnp.bfloat16)


def column(rank, values):
    n_blocks = rank.shape[0]
    slot = (iota((n_blocks, CAP, LANES), 1) + 1).astype(F32)
    v = jnp.where(rank[:, None, :] == slot, values[:, None, :], F32(0))
    return jnp.sum(v, axis=2, keepdims=True).reshape(n_blocks * CAP, 1)


def scatter_source(weights, ranks, hot_z, hot_row, source):
    @pl.loop(0, len(SLABS), unroll=len(SLABS))
    def _(s):
        put = jnp.concatenate(
            [hot_z[s] * column(ranks[s], weights[:, part, :]) for part in range(2)], axis=1
        )
        grid = None
        for _ in range(3):
            piece = put.astype(jnp.bfloat16)
            put = put - piece.astype(F32)
            term = jnp.dot(hot_row[s], piece, preferred_element_type=F32)
            grid = term if grid is None else grid + term
        for part in range(2):
            for comp in range(3):
                for plane in range(2):
                    row = comp * 64 + plane * 32
                    source[3 * part + comp, 2 * s + plane] = grid[
                        row : row + 32, part * LANES : (part + 1) * LANES
                    ]


def into(ref):
    def store(part, comp, at, value):
        ref[3 * part + comp, at] = value

    return store


def place_kernel(
    n_slabs, slab_of, cell_of, comp_of, freqs, pair, ranks, hot_z, hot_row, wave
):
    me = lax.axis_index("space")
    wave[...] = jnp.full(BLK, freqs[pair[0]], F32)
    place_measurements(me, n_slabs, slab_of, cell_of, comp_of, ranks, hot_z, hot_row)


def start_kernel(
    own, b2, b1, a1, a2, a3, weights, ranks, hot_z, hot_row, wave,
    p0_out, p1_out, p2_out, damp_out, gram_out,
    field, damping, source, p0, p1,
):
    me = lax.axis_index("space")
    for s, ref in enumerate((b2, b1, own, a1, a2, a3)):
        for k in range(6):
            field[k, 2 * s : 2 * s + 2] = ref[2 * k : 2 * k + 2]
        damping[2 * s : 2 * s + 2] = ref[12:14] * wave[0:1, :]
    scatter_source(weights, ranks, hot_z, hot_row, source)

    def keep_p0(part, comp, at, value):
        p0[3 * part + comp, at] = source[3 * part + comp, at] - value

    def keep_p2(part, comp, at, value):
        p2_out[3 * part + comp, at - 3] = value

    apply(me, field, damping, -4, 1, 11, keep_p0, 5)
    apply(me, p0, damping, -4, 2, 10, into(p1), 4)
    apply(me, p1, damping, -4, 3, 9, keep_p2, 3)
    for k in range(6):
        p0_out[k] = p0[k, 3:9]
        p1_out[k] = p1[k, 3:9]
    damp_out[...] = damping[3:9]
    gram(((p0, 5), (p1, 5), (p2_out, 2)), PAIRS_1, gram_out)


def middle_kernel(
    parts, p0, p1, p2, damping, own,
    xs_out, r_out, d_out, m_out, f_out, gram_out,
    r, m, f, g, h,
):
    me = lax.axis_index("space")
    e = gathered(parts, PAIRS_1)
    den = e[1, 1][0][0]
    a = over(e[1, 0], den)
    t = csum([e[1, 1], mix(e[1, 2], cneg(a))])
    b = cneg(over(t, den))
    u = (F32(1) + b[0], b[1])
    w = [conj(csum([mix(e[i, 1], u), mix(e[i, 2], cneg(a))])) for i in range(3)]
    num = csum([w[0], mix(w[1], cneg(a))])
    den = pair_add(mix_re(w[1], u), mix_re(w[2], cneg(a)))[0]
    step = over(num, den)
    su = cmul(step, u)
    s = (a[0] + su[0], a[1] + su[1])
    v = cmul(step, a)
    a, u, s, v = rows(a), rows(u), rows(s), rows(v)

    @pl.loop(0, 6)
    def _(at):
        for c in range(3):
            v0 = (p0[c, at], p0[3 + c, at])
            v1 = (p1[c, at], p1[3 + c, at])
            v2 = (p2[c, at], p2[3 + c, at])
            s1, w2 = scaled(s, *v1), scaled(v, *v2)
            u1, a2 = scaled(u, *v1), scaled(a, *v2)
            for part in range(2):
                r[3 * part + c, at] = (v0[part] - s1[part]) + w2[part]
                m[3 * part + c, at] = u1[part] - a2[part]

    for plane in range(2):
        for c in range(3):
            v0 = (p0[c, 1 + plane], p0[3 + c, 1 + plane])
            v1 = (p1[c, 1 + plane], p1[3 + c, 1 + plane])
            s0, w1 = scaled(s, *v0), scaled(v, *v1)
            u0, a1 = scaled(u, *v0), scaled(a, *v1)
            for part in range(2):
                k = 2 * (3 * part + c) + plane
                xs_out[k] = (own[k] + s0[part]) - w1[part]
                d_out[k] = u0[part] - a1[part]
                r_out[k] = r[3 * part + c, 1 + plane]
                m_out[k] = m[3 * part + c, 1 + plane]

    apply(me, r, damping, -1, 1, 5, into(f))
    apply(me, m, damping, -1, 2, 4, into(g))
    apply(me, f, damping, -1, 2, 4, into(h))
    for k in range(6):
        f_out[2 * k : 2 * k + 2] = f[k, 1:3]
    gram(((r, 2), (m, 2), (f, 2), (g, 2), (h, 2)), PAIRS_2, gram_out)


def end_kernel(parts, xs, r, d, m, f, background, wave, adjoint_out, terms_out):
    e = gathered(parts, PAIRS_2)
    b = cneg(over(e[1, 2], e[1, 1][0][0]))
    w = [conj(csum([mix(e[i, 1], b), e[i, 2]])) for i in range(5)]
    den = pair_add(mix_re(w[1], b), w[2][0])[0]
    a = over(w[0], den)
    ab = cmul(a, b)
    t = csum([w[2], mix(w[3], cneg(ab)), mix(w[4], cneg(a))])
    b2 = cneg(over(t, den))
    q1, q2 = (F32(1) + b2[0], b2[1]), cmul(b2, b)
    mapped = (q2, q1, cneg(ab), cneg(a))
    w = [conj(csum([mix(e[i, 1 + k], q) for k, q in enumerate(mapped)])) for i in range(5)]
    num = csum([w[0], mix(w[1], cneg(ab)), mix(w[2], cneg(a))])
    den = total([mix_re(w[1 + k], q) for k, q in enumerate(mapped)])[0]
    a2 = over(num, den)
    to_r, to_d = cmul(a2, q1), cmul(a2, q2)
    to_r = rows((a[0] + to_r[0], a[1] + to_r[1]))
    to_d = rows((ab[0] + to_d[0], ab[1] + to_d[1]))
    to_f, to_m = rows(cmul(a2, a)), rows(cmul(a2, ab))
    for plane in range(2):
        terms = jnp.zeros((ROWS, LANES), F32)
        for c in range(3):
            k, q = 2 * c + plane, 2 * (3 + c) + plane
            add = [
                scaled(to_r, r[k], r[q]),
                scaled(to_d, d[k], d[q]),
                cneg(scaled(to_f, f[k], f[q])),
                cneg(scaled(to_m, m[k], m[q])),
            ]
            re = xs[k] + ((add[0][0] + add[1][0]) + (add[2][0] + add[3][0]))
            im = xs[q] + ((add[0][1] + add[1][1]) + (add[2][1] + add[3][1]))
            adjoint_out[k] = re
            adjoint_out[q] = im
            terms = terms + (re * background[q] + im * background[k])
        terms = terms * wave[0:1, :]
        n_src = terms_out.shape[0]
        part = ROWS // n_src
        for n in range(n_src):
            terms_out[n, plane * part : (plane + 1) * part] = terms[n * part : (n + 1) * part]


def shaped(*shape):
    return jax.ShapeDtypeStruct(shape, F32)


def kernel(body, name, in_specs, outs, scratch, flops):
    return pl.pallas_call(
        body,
        name=name,
        in_specs=in_specs,
        out_specs=tuple(spec() for _ in outs),
        out_shape=tuple(outs),
        scratch_shapes=[pltpu.VMEM(s, F32) for s in scratch],
        compiler_params=pltpu.CompilerParams(vmem_limit_bytes=VMEM_BYTES),
        cost_estimate=pl.CostEstimate(flops=flops, bytes_accessed=3_000_000, transcendentals=0),
    )


def shards(
    background,
    warm_start,
    conductivity,
    frequencies,
    pair_freq,
    weighted_residual,
    datum_layer_index,
    receiver_flat_cell,
    receiver_component,
):
    n_slabs, n_src = lax.axis_size("space"), lax.axis_size("src")
    own = warm_start.reshape(12, ROWS, LANES)
    message = jnp.concatenate([own, conductivity], axis=0)

    def from_slab(away):
        route = [((i + away) % n_slabs, i) for i in range(n_slabs)]
        return lax.ppermute(message, "space", route)

    window = [from_slab(away) for away in (-2, -1, 1, 2, 3)]
    weights = jnp.broadcast_to(weighted_residual.reshape(1, 2, LANES), (n_slabs, 2, LANES))
    weights = lax.all_to_all(weights, "space", split_axis=0, concat_axis=0, tiled=True)
    plane = (ROWS, LANES)
    slab_of = datum_layer_index.reshape(n_slabs, LANES)
    cell_of = receiver_flat_cell.reshape(n_slabs, LANES)
    comp_of = receiver_component.reshape(n_slabs, LANES)
    smem = spec(pltpu.SMEM)
    six = shaped(6, 6, *plane)
    slots = n_slabs * CAP
    places = kernel(
        functools.partial(place_kernel, n_slabs),
        "place",
        [spec()] * 3 + [smem] * 2,
        [
            shaped(len(SLABS), *plane),
            shaped(len(SLABS), slots, LANES),
            jax.ShapeDtypeStruct((len(SLABS), 256, slots), jnp.bfloat16),
            shaped(*BLK),
        ],
        [],
        20_000_000,
    )(slab_of, cell_of, comp_of, frequencies, pair_freq)
    wave = places[-1]
    p0, p1, p2, damping, parts = kernel(
        start_kernel,
        "start",
        [spec()] * 11,
        [six, six, six, shaped(6, *plane), shaped(n_slabs, LANES)],
        [(6, 12, *plane), (12, *plane), (6, 12, *plane), (6, 12, *plane), (6, 12, *plane)],
        40_000_000,
    )(message, *window, weights, *places)
    parts = lax.all_to_all(parts, "space", split_axis=0, concat_axis=0, tiled=True)
    two = shaped(12, *plane)
    xs, r, d, m, f, parts = kernel(
        middle_kernel,
        "middle",
        [spec()] * 6,
        [two] * 5 + [shaped(n_slabs, LANES)],
        [(6, 6, *plane)] * 5,
        40_000_000,
    )(parts, p0, p1, p2, damping, own)
    parts = lax.all_to_all(parts, "space", split_axis=0, concat_axis=0, tiled=True)
    adjoint, terms = kernel(
        end_kernel,
        "end",
        [spec()] * 8,
        [two, shaped(n_src, 2 * (ROWS // n_src), LANES)],
        [],
        5_000_000,
    )(parts, xs, r, d, m, f, background.reshape(12, *plane), wave)
    terms = lax.all_to_all(terms, "src", split_axis=0, concat_axis=0, tiled=True)
    gradient = jnp.sum(terms, axis=0).reshape(2, ROWS // n_src, LANES)
    return adjoint.reshape(warm_start.shape), gradient


def solution(mesh):
    placed = (
        P(None, "src", None, "space", None, None),
        P(None, "src", None, "space", None, None),
        P("space", None, None),
        P(),
        P("src"),
        P(None, "src", "space"),
        P(),
        P(),
        P(),
    )
    return jax.shard_map(
        shards,
        mesh=mesh,
        in_specs=placed,
        out_specs=(P(None, "src", None, "space", None, None), P("space", "src", None)),
        check_vma=False,
    )
```

```python
import functools

import jax
import jax.numpy as jnp
from jax import lax
from jax.experimental import pallas as pl
from jax.experimental.pallas import tpu as pltpu
from jax.sharding import PartitionSpec as P

F32 = jnp.float32
SLABS = (-2, -1, 0, 1, 2, 3)
ROWS, LANES = 32, 128
BLK = (8, 128)
CAP = 8
VMEM_BYTES = 14 * 1024 * 1024


def spec(space=pltpu.VMEM):
    return pl.BlockSpec(memory_space=space)


def iota(shape, axis):
    return lax.broadcasted_iota(jnp.int32, shape, axis)


def two_sum(a, b):
    s = a + b
    t = s - a
    return s, (a - (s - t)) + (b - t)


def split(a):
    t = a * F32(4097.0)
    high = t - (t - a)
    return high, a - high


def product_error(p, a, b):
    (ah, al), (bh, bl) = a, b
    return ((ah * bh - p) + ah * bl + al * bh) + al * bl


def pair_add(a, b):
    s, e = two_sum(a[0], b[0])
    e = e + (a[1] + b[1])
    h = s + e
    return h, e - (h - s)


def pair_scale(a, c):
    p = a[0] * c
    e = product_error(p, split(a[0]), split(c)) + a[1] * c
    h = p + e
    return h, e - (h - p)


def negate(a):
    return tuple(-v for v in a)


def total(terms):
    return functools.reduce(pair_add, terms)


def mix_re(g, v):
    return pair_add(pair_scale(g[0], v[0]), negate(pair_scale(g[1], v[1])))


def mix(g, v):
    return mix_re(g, v), pair_add(pair_scale(g[0], v[1]), pair_scale(g[1], v[0]))


def csum(terms):
    return total([t[0] for t in terms]), total([t[1] for t in terms])


def conj(g):
    return g[0], negate(g[1])


def cneg(v):
    return -v[0], -v[1]


def cmul(a, b):
    return a[0] * b[0] - a[1] * b[1], a[0] * b[1] + a[1] * b[0]


def over(g, den):
    return g[0][0] / den, g[1][0] / den


def y_next(e):
    return jnp.where(iota(e.shape, 0) == ROWS - 1, F32(0), pltpu.roll(e, ROWS - 1, 0))


def z_next(e):
    return jnp.where(iota(e.shape, 1) == LANES - 1, F32(0), pltpu.roll(e, LANES - 1, 1))


def y_prev(h, first):
    return jnp.where(iota(h.shape, 0) == 0, first, pltpu.roll(h, 1, 0))


def z_prev(h, first):
    return jnp.where(iota(h.shape, 1) == 0, first, pltpu.roll(h, 1, 1))


def forward_yz(ex, ey, ez, ey_up, ez_up):
    hy = (z_next(ex) - ex) - (ez_up - ez)
    hz = (ey_up - ey) - (y_next(ex) - ex)
    return hy, hz


def curl_curl(field, part, at, above, below, before):
    ex, ey, ez = (field[3 * part + c, at] for c in range(3))
    ey_up, ez_up = (field[3 * part + c, at + 1] * above for c in (1, 2))
    hx = (y_next(ez) - ez) - (z_next(ey) - ey)
    hy, hz = forward_yz(ex, ey, ez, ey_up, ez_up)
    edge = F32(1) - below
    hy_dn = before[0] * below - ez * edge
    hz_dn = before[1] * below + ey * edge
    result = (
        (hz - y_prev(hz, -ex)) - (hy - z_prev(hy, ex)),
        (hx - z_prev(hx, -ey)) - (hz - hz_dn),
        (hy - hy_dn) - (hx - y_prev(hx, ez)),
    )
    return result, (hy, hz)


def apply(me, field, damping, first, low, high, store, unroll=2):
    def plane(at, before):
        grid_plane = lax.rem(2 * me + first + at + 64, 64)
        above = jnp.where(grid_plane == 63, F32(0), F32(1))
        below = jnp.where(grid_plane == 0, F32(0), F32(1))
        damp = damping[at]
        real, real_h = curl_curl(field, 0, at, above, below, before[:2])
        for c in range(3):
            store(0, c, at, real[c] - damp * field[3 + c, at])
        imag, imag_h = curl_curl(field, 1, at, above, below, before[2:])
        for c in range(3):
            store(1, c, at, imag[c] + damp * field[c, at])
        return real_h + imag_h

    below_first = []
    for part in range(2):
        under = [field[3 * part + c, low - 1] for c in range(3)]
        below_first += forward_yz(*under, *(field[3 * part + c, low] for c in (1, 2)))
    lax.fori_loop(low, high, plane, tuple(below_first), unroll=unroll)


def gram(fields, pairs, out, spare, size=14):
    names = sorted({k for pair in pairs for k in pair})

    def block(step, k, part):
        comp, rest = step // 8, lax.rem(step, 8)
        plane, row = rest // 4, pl.multiple_of(lax.rem(rest, 4) * 8, 8)
        ref, start = fields[k]
        return ref[3 * part + comp, start + plane, pl.ds(row, 8), :]

    def peak(step, tops):
        return tuple(
            jnp.maximum(top, jnp.maximum(jnp.abs(block(step, k, 0)), jnp.abs(block(step, k, 1))))
            for k, top in zip(names, tops)
        )

    zero = jnp.zeros(BLK, F32)
    tops = lax.fori_loop(0, 24, peak, tuple(zero for _ in names), unroll=6)
    grids = {k: top * F32(2.0**15) for k, top in zip(names, tops)}
    sums = []
    for first in range(0, len(pairs), size):
        group = pairs[first : first + size]
        used = sorted({k for pair in group for k in pair})
        count = sum(1 if i == j else 2 for i, j in group)

        def body(step, acc, group=group, used=used):
            values = {}
            for k in used:
                for part in range(2):
                    v = block(step, k, part)
                    high = (v + grids[k]) - grids[k]
                    values[k, part] = v, high, v - high

            def products(a, b):
                return a[1] * b[1], a[1] * b[2] + a[2] * b[0]

            new = []
            for i, j in group:
                x, y = products(values[i, 0], values[j, 0]), products(values[i, 1], values[j, 1])
                re = acc[len(new)]
                new.append(tuple(re[n] + (x[n] + y[n]) for n in range(2)))
                if i != j:
                    x, y = products(values[i, 0], values[j, 1]), products(values[i, 1], values[j, 0])
                    im = acc[len(new)]
                    new.append(tuple(im[n] + (x[n] - y[n]) for n in range(2)))
            return tuple(new)

        sums += list(
            lax.fori_loop(0, 24, body, tuple((zero, zero) for _ in range(count)), unroll=6)
        )
    count = len(sums)
    for k, s in enumerate(sums):
        for n in range(2):
            spare[n, 8 * k : 8 * k + 8, :] = s[n]
    lines = [tuple(spare[n, pl.ds(row, count, stride=8), :] for n in range(2)) for row in range(8)]
    while len(lines) > 1:
        lines = [pair_add(x, y) for x, y in zip(lines[::2], lines[1::2])]
    s = lines[0]
    for shift in (64, 32, 16, 8, 4, 2, 1):
        s = pair_add(s, tuple(pltpu.roll(v, shift, 1) for v in s))
    away = iota(s[0].shape, 1) - iota(s[0].shape, 0)
    line = jnp.where(away == 0, s[0], F32(0)) + jnp.where(away == 64, s[1], F32(0))
    line = jnp.sum(line, axis=0, keepdims=True)
    out[...] = jnp.broadcast_to(line, out.shape)


def gathered(parts, pairs):
    lines = []
    for n in range(parts.shape[0] // 8):
        high = parts[8 * n : 8 * n + 8, :]
        lines.append((high, pltpu.roll(high, 64, 1)))
    s = total(lines)
    for shift in (4, 2, 1):
        s = pair_add(s, tuple(pltpu.roll(v, shift, 0) for v in s))
    entries, at = {}, 0

    def lane(k):
        return tuple(jnp.broadcast_to(v[:, k : k + 1], BLK) for v in s)

    zero = (jnp.zeros(BLK, F32), jnp.zeros(BLK, F32))
    for i, j in pairs:
        re, at = lane(at), at + 1
        im = zero
        if i != j:
            im, at = lane(at), at + 1
        entries[i, j] = (re, im)
        entries[j, i] = (re, negate(im)) if i != j else (re, im)
    return entries


def rows(v):
    return tuple(jnp.concatenate([x] * (ROWS // 8), axis=0) for x in v)


def scaled(v, re, im):
    return v[0] * re - v[1] * im, v[0] * im + v[1] * re


PAIRS_1 = ((1, 1), (2, 2), (0, 1), (1, 2), (0, 2))
PAIRS_2 = ((1, 1), (2, 2), (3, 3), (4, 4), (0, 1), (0, 2), (1, 2), (0, 3), (0, 4), (1, 3), (1, 4), (2, 3), (2, 4), (3, 4))


def place_measurements(me, n_slabs, slab_of, cell_of, comp_of, ranks, hot_z, hot_row):
    upper = (iota((LANES, LANES), 0) <= iota((LANES, LANES), 1)).astype(jnp.bfloat16)
    key = (comp_of[...] * 8192 + cell_of[...]).astype(F32)
    n_blocks = key.shape[0]
    slots = n_blocks * CAP
    same = (iota((slots, slots), 0) == iota((slots, slots), 1)).astype(jnp.bfloat16)

    @pl.loop(0, len(SLABS))
    def _(s):
        slab = lax.rem(me + s + SLABS[0] + n_slabs, n_slabs)
        mine = slab_of[...] == slab
        mine_f = jnp.where(mine, F32(1), F32(0))
        rank = jnp.dot(mine_f.astype(jnp.bfloat16), upper, preferred_element_type=F32)
        rank = jnp.where(mine, rank, F32(0))
        ranks[s] = rank
        place = column(rank, key).astype(jnp.int32)
        at_z = (place & (LANES - 1)) == iota((slots, LANES), 1)
        hot_z[s] = jnp.where(at_z, F32(1), F32(0))
        at_row = jnp.where((place >> 7) == iota((slots, 256), 1), F32(1), F32(0))
        turned = lax.dot_general(
            at_row.astype(jnp.bfloat16), same, (((0,), (0,)), ((), ())), preferred_element_type=F32
        )
        hot_row[s] = turned.astype(jnp.bfloat16)


def column(rank, values):
    n_blocks = rank.shape[0]
    slot = (iota((n_blocks, CAP, LANES), 1) + 1).astype(F32)
    v = jnp.where(rank[:, None, :] == slot, values[:, None, :], F32(0))
    return jnp.sum(v, axis=2, keepdims=True).reshape(n_blocks * CAP, 1)


def scatter_source(weights, ranks, hot_z, hot_row, source):
    @pl.loop(0, len(SLABS), unroll=len(SLABS))
    def _(s):
        put = jnp.concatenate(
            [hot_z[s] * column(ranks[s], weights[:, part, :]) for part in range(2)], axis=1
        )
        grid = None
        for _ in range(3):
            piece = put.astype(jnp.bfloat16)
            put = put - piece.astype(F32)
            term = jnp.dot(hot_row[s], piece, preferred_element_type=F32)
            grid = term if grid is None else grid + term
        for part in range(2):
            for comp in range(3):
                for plane in range(2):
                    row = comp * 64 + plane * 32
                    source[3 * part + comp, 2 * s + plane] = grid[
                        row : row + 32, part * LANES : (part + 1) * LANES
                    ]


def into(ref):
    def store(part, comp, at, value):
        ref[3 * part + comp, at] = value

    return store


def place_kernel(
    n_slabs, slab_of, cell_of, comp_of, freqs, pair, ranks, hot_z, hot_row, wave
):
    me = lax.axis_index("space")
    wave[...] = jnp.full(BLK, freqs[pair[0]], F32)
    place_measurements(me, n_slabs, slab_of, cell_of, comp_of, ranks, hot_z, hot_row)


def start_kernel(
    own, b2, b1, a1, a2, a3, weights, ranks, hot_z, hot_row, wave,
    p0_out, p1_out, p2_out, damp_out, gram_out,
    field, damping, source, p0, p1, spare,
):
    me = lax.axis_index("space")
    for s, ref in enumerate((b2, b1, own, a1, a2, a3)):
        for k in range(6):
            field[k, 2 * s : 2 * s + 2] = ref[2 * k : 2 * k + 2]
        damping[2 * s : 2 * s + 2] = ref[12:14] * wave[0:1, :]
    scatter_source(weights, ranks, hot_z, hot_row, source)

    def keep_p0(part, comp, at, value):
        p0[3 * part + comp, at] = source[3 * part + comp, at] - value

    def keep_p2(part, comp, at, value):
        p2_out[3 * part + comp, at - 3] = value

    apply(me, field, damping, -4, 1, 11, keep_p0, 5)
    apply(me, p0, damping, -4, 2, 10, into(p1), 4)
    apply(me, p1, damping, -4, 3, 9, keep_p2, 3)
    for k in range(6):
        p0_out[k] = p0[k, 3:9]
        p1_out[k] = p1[k, 3:9]
    damp_out[...] = damping[3:9]
    gram(((p0, 5), (p1, 5), (p2_out, 2)), PAIRS_1, gram_out, spare)


def middle_kernel(
    parts, p0, p1, p2, damping, own,
    xs_out, r_out, d_out, m_out, f_out, gram_out,
    r, m, f, g, h, spare,
):
    me = lax.axis_index("space")
    e = gathered(parts, PAIRS_1)
    den = e[1, 1][0][0]
    a = over(e[1, 0], den)
    t = csum([e[1, 1], mix(e[1, 2], cneg(a))])
    b = cneg(over(t, den))
    u = (F32(1) + b[0], b[1])
    w = [conj(csum([mix(e[i, 1], u), mix(e[i, 2], cneg(a))])) for i in range(3)]
    num = csum([w[0], mix(w[1], cneg(a))])
    den = pair_add(mix_re(w[1], u), mix_re(w[2], cneg(a)))[0]
    step = over(num, den)
    su = cmul(step, u)
    s = (a[0] + su[0], a[1] + su[1])
    v = cmul(step, a)
    a, u, s, v = rows(a), rows(u), rows(s), rows(v)

    @pl.loop(0, 6)
    def _(at):
        for c in range(3):
            v0 = (p0[c, at], p0[3 + c, at])
            v1 = (p1[c, at], p1[3 + c, at])
            v2 = (p2[c, at], p2[3 + c, at])
            s1, w2 = scaled(s, *v1), scaled(v, *v2)
            u1, a2 = scaled(u, *v1), scaled(a, *v2)
            for part in range(2):
                r[3 * part + c, at] = (v0[part] - s1[part]) + w2[part]
                m[3 * part + c, at] = u1[part] - a2[part]

    for plane in range(2):
        for c in range(3):
            v0 = (p0[c, 1 + plane], p0[3 + c, 1 + plane])
            v1 = (p1[c, 1 + plane], p1[3 + c, 1 + plane])
            s0, w1 = scaled(s, *v0), scaled(v, *v1)
            u0, a1 = scaled(u, *v0), scaled(a, *v1)
            for part in range(2):
                k = 2 * (3 * part + c) + plane
                xs_out[k] = (own[k] + s0[part]) - w1[part]
                d_out[k] = u0[part] - a1[part]
                r_out[k] = r[3 * part + c, 1 + plane]
                m_out[k] = m[3 * part + c, 1 + plane]

    apply(me, r, damping, -1, 1, 5, into(f))
    apply(me, m, damping, -1, 2, 4, into(g))
    apply(me, f, damping, -1, 2, 4, into(h))
    for k in range(6):
        f_out[2 * k : 2 * k + 2] = f[k, 1:3]
    gram(((r, 2), (m, 2), (f, 2), (g, 2), (h, 2)), PAIRS_2, gram_out, spare)


def end_kernel(parts, xs, r, d, m, f, background, wave, adjoint_out, terms_out):
    e = gathered(parts, PAIRS_2)
    b = cneg(over(e[1, 2], e[1, 1][0][0]))
    w = [conj(csum([mix(e[i, 1], b), e[i, 2]])) for i in range(5)]
    den = pair_add(mix_re(w[1], b), w[2][0])[0]
    a = over(w[0], den)
    ab = cmul(a, b)
    t = csum([w[2], mix(w[3], cneg(ab)), mix(w[4], cneg(a))])
    b2 = cneg(over(t, den))
    q1, q2 = (F32(1) + b2[0], b2[1]), cmul(b2, b)
    mapped = (q2, q1, cneg(ab), cneg(a))
    w = [conj(csum([mix(e[i, 1 + k], q) for k, q in enumerate(mapped)])) for i in range(5)]
    num = csum([w[0], mix(w[1], cneg(ab)), mix(w[2], cneg(a))])
    den = total([mix_re(w[1 + k], q) for k, q in enumerate(mapped)])[0]
    a2 = over(num, den)
    to_r, to_d = cmul(a2, q1), cmul(a2, q2)
    to_r = rows((a[0] + to_r[0], a[1] + to_r[1]))
    to_d = rows((ab[0] + to_d[0], ab[1] + to_d[1]))
    to_f, to_m = rows(cmul(a2, a)), rows(cmul(a2, ab))
    for plane in range(2):
        terms = jnp.zeros((ROWS, LANES), F32)
        for c in range(3):
            k, q = 2 * c + plane, 2 * (3 + c) + plane
            add = [
                scaled(to_r, r[k], r[q]),
                scaled(to_d, d[k], d[q]),
                cneg(scaled(to_f, f[k], f[q])),
                cneg(scaled(to_m, m[k], m[q])),
            ]
            re = xs[k] + ((add[0][0] + add[1][0]) + (add[2][0] + add[3][0]))
            im = xs[q] + ((add[0][1] + add[1][1]) + (add[2][1] + add[3][1]))
            adjoint_out[k] = re
            adjoint_out[q] = im
            terms = terms + (re * background[q] + im * background[k])
        terms = terms * wave[0:1, :]
        n_src = terms_out.shape[0]
        part = ROWS // n_src
        for n in range(n_src):
            terms_out[n, plane * part : (plane + 1) * part] = terms[n * part : (n + 1) * part]


def shaped(*shape):
    return jax.ShapeDtypeStruct(shape, F32)


def kernel(body, name, in_specs, outs, scratch, flops):
    return pl.pallas_call(
        body,
        name=name,
        in_specs=in_specs,
        out_specs=tuple(spec() for _ in outs),
        out_shape=tuple(outs),
        scratch_shapes=[pltpu.VMEM(s, F32) for s in scratch],
        compiler_params=pltpu.CompilerParams(vmem_limit_bytes=VMEM_BYTES),
        cost_estimate=pl.CostEstimate(flops=flops, bytes_accessed=3_000_000, transcendentals=0),
    )


def shards(
    background,
    warm_start,
    conductivity,
    frequencies,
    pair_freq,
    weighted_residual,
    datum_layer_index,
    receiver_flat_cell,
    receiver_component,
):
    n_slabs, n_src = lax.axis_size("space"), lax.axis_size("src")
    own = warm_start.reshape(12, ROWS, LANES)
    message = jnp.concatenate([own, conductivity], axis=0)

    def from_slab(away):
        route = [((i + away) % n_slabs, i) for i in range(n_slabs)]
        return lax.ppermute(message, "space", route)

    window = [from_slab(away) for away in (-2, -1, 1, 2, 3)]
    weights = jnp.broadcast_to(weighted_residual.reshape(1, 2, LANES), (n_slabs, 2, LANES))
    weights = lax.all_to_all(weights, "space", split_axis=0, concat_axis=0, tiled=True)
    plane = (ROWS, LANES)
    slab_of = datum_layer_index.reshape(n_slabs, LANES)
    cell_of = receiver_flat_cell.reshape(n_slabs, LANES)
    comp_of = receiver_component.reshape(n_slabs, LANES)
    smem = spec(pltpu.SMEM)
    six = shaped(6, 6, *plane)
    slots = n_slabs * CAP
    places = kernel(
        functools.partial(place_kernel, n_slabs),
        "place",
        [spec()] * 3 + [smem] * 2,
        [
            shaped(len(SLABS), *plane),
            shaped(len(SLABS), slots, LANES),
            jax.ShapeDtypeStruct((len(SLABS), 256, slots), jnp.bfloat16),
            shaped(*BLK),
        ],
        [],
        20_000_000,
    )(slab_of, cell_of, comp_of, frequencies, pair_freq)
    wave = places[-1]
    p0, p1, p2, damping, parts = kernel(
        start_kernel,
        "start",
        [spec()] * 11,
        [six, six, six, shaped(6, *plane), shaped(n_slabs, LANES)],
        [(6, 12, *plane), (12, *plane), *[(6, 12, *plane)] * 3, (2, 64, LANES)],
        40_000_000,
    )(message, *window, weights, *places)
    parts = lax.all_to_all(parts, "space", split_axis=0, concat_axis=0, tiled=True)
    two = shaped(12, *plane)
    xs, r, d, m, f, parts = kernel(
        middle_kernel,
        "middle",
        [spec()] * 6,
        [two] * 5 + [shaped(n_slabs, LANES)],
        [(6, 6, *plane)] * 5 + [(2, 192, LANES)],
        40_000_000,
    )(parts, p0, p1, p2, damping, own)
    parts = lax.all_to_all(parts, "space", split_axis=0, concat_axis=0, tiled=True)
    adjoint, terms = kernel(
        end_kernel,
        "end",
        [spec()] * 8,
        [two, shaped(n_src, 2 * (ROWS // n_src), LANES)],
        [],
        5_000_000,
    )(parts, xs, r, d, m, f, background.reshape(12, *plane), wave)
    terms = lax.all_to_all(terms, "src", split_axis=0, concat_axis=0, tiled=True)
    gradient = jnp.sum(terms, axis=0).reshape(2, ROWS // n_src, LANES)
    return adjoint.reshape(warm_start.shape), gradient


def solution(mesh):
    placed = (
        P(None, "src", None, "space", None, None),
        P(None, "src", None, "space", None, None),
        P("space", None, None),
        P(),
        P("src"),
        P(None, "src", "space"),
        P(),
        P(),
        P(),
    )
    return jax.shard_map(
        shards,
        mesh=mesh,
        in_specs=placed,
        out_specs=(P(None, "src", None, "space", None, None), P("space", "src", None)),
        check_vma=False,
    )
```

```python
import functools

import jax
import jax.numpy as jnp
from jax import lax
from jax.experimental import pallas as pl
from jax.experimental.pallas import tpu as pltpu
from jax.sharding import PartitionSpec as P

F32 = jnp.float32
SLABS = (-2, -1, 0, 1, 2, 3)
ROWS, LANES = 32, 128
BLK = (8, 128)
CAP = 8
VMEM_BYTES = 14 * 1024 * 1024


def spec(space=pltpu.VMEM):
    return pl.BlockSpec(memory_space=space)


def iota(shape, axis):
    return lax.broadcasted_iota(jnp.int32, shape, axis)


def two_sum(a, b):
    s = a + b
    t = s - a
    return s, (a - (s - t)) + (b - t)


def split(a):
    t = a * F32(4097.0)
    high = t - (t - a)
    return high, a - high


def product_error(p, a, b):
    (ah, al), (bh, bl) = a, b
    return ((ah * bh - p) + ah * bl + al * bh) + al * bl


def pair_add(a, b):
    s, e = two_sum(a[0], b[0])
    e = e + (a[1] + b[1])
    h = s + e
    return h, e - (h - s)


def pair_scale(a, c):
    p = a[0] * c
    e = product_error(p, split(a[0]), split(c)) + a[1] * c
    h = p + e
    return h, e - (h - p)


def negate(a):
    return tuple(-v for v in a)


def total(terms):
    return functools.reduce(pair_add, terms)


def mix_re(g, v):
    return pair_add(pair_scale(g[0], v[0]), negate(pair_scale(g[1], v[1])))


def mix(g, v):
    return mix_re(g, v), pair_add(pair_scale(g[0], v[1]), pair_scale(g[1], v[0]))


def csum(terms):
    return total([t[0] for t in terms]), total([t[1] for t in terms])


def conj(g):
    return g[0], negate(g[1])


def cneg(v):
    return -v[0], -v[1]


def cmul(a, b):
    return a[0] * b[0] - a[1] * b[1], a[0] * b[1] + a[1] * b[0]


def over(g, den):
    return g[0][0] / den, g[1][0] / den


def y_next(e):
    return jnp.where(iota(e.shape, 0) == ROWS - 1, F32(0), pltpu.roll(e, ROWS - 1, 0))


def z_next(e):
    return jnp.where(iota(e.shape, 1) == LANES - 1, F32(0), pltpu.roll(e, LANES - 1, 1))


def y_prev(h, first):
    return jnp.where(iota(h.shape, 0) == 0, first, pltpu.roll(h, 1, 0))


def z_prev(h, first):
    return jnp.where(iota(h.shape, 1) == 0, first, pltpu.roll(h, 1, 1))


def forward_yz(ex, ey, ez, ey_up, ez_up):
    hy = (z_next(ex) - ex) - (ez_up - ez)
    hz = (ey_up - ey) - (y_next(ex) - ex)
    return hy, hz


def curl_curl(field, part, at, above, below, before):
    ex, ey, ez = (field[3 * part + c, at] for c in range(3))
    ey_up, ez_up = (field[3 * part + c, at + 1] * above for c in (1, 2))
    hx = (y_next(ez) - ez) - (z_next(ey) - ey)
    hy, hz = forward_yz(ex, ey, ez, ey_up, ez_up)
    edge = F32(1) - below
    hy_dn = before[0] * below - ez * edge
    hz_dn = before[1] * below + ey * edge
    result = (
        (hz - y_prev(hz, -ex)) - (hy - z_prev(hy, ex)),
        (hx - z_prev(hx, -ey)) - (hz - hz_dn),
        (hy - hy_dn) - (hx - y_prev(hx, ez)),
    )
    return result, (hy, hz)


def apply(me, field, damping, first, low, high, store, unroll=2):
    def plane(at, before):
        grid_plane = lax.rem(2 * me + first + at + 64, 64)
        above = jnp.where(grid_plane == 63, F32(0), F32(1))
        below = jnp.where(grid_plane == 0, F32(0), F32(1))
        damp = damping[at]
        real, real_h = curl_curl(field, 0, at, above, below, before[:2])
        for c in range(3):
            store(0, c, at, real[c] - damp * field[3 + c, at])
        imag, imag_h = curl_curl(field, 1, at, above, below, before[2:])
        for c in range(3):
            store(1, c, at, imag[c] + damp * field[c, at])
        return real_h + imag_h

    below_first = []
    for part in range(2):
        under = [field[3 * part + c, low - 1] for c in range(3)]
        below_first += forward_yz(*under, *(field[3 * part + c, low] for c in (1, 2)))
    lax.fori_loop(low, high, plane, tuple(below_first), unroll=unroll)


def gram(fields, pairs, out, spare, size=14):
    names = sorted({k for pair in pairs for k in pair})

    def block(step, k, part):
        comp, rest = step // 8, lax.rem(step, 8)
        plane, row = rest // 4, pl.multiple_of(lax.rem(rest, 4) * 8, 8)
        ref, start = fields[k]
        return ref[3 * part + comp, start + plane, pl.ds(row, 8), :]

    def peak(step, tops):
        return tuple(
            jnp.maximum(top, jnp.maximum(jnp.abs(block(step, k, 0)), jnp.abs(block(step, k, 1))))
            for k, top in zip(names, tops)
        )

    zero = jnp.zeros(BLK, F32)
    tops = lax.fori_loop(0, 24, peak, tuple(zero for _ in names), unroll=6)
    grids = {k: top * F32(2.0**15) for k, top in zip(names, tops)}
    sums = []
    for first in range(0, len(pairs), size):
        group = pairs[first : first + size]
        used = sorted({k for pair in group for k in pair})
        count = sum(1 if i == j else 2 for i, j in group)

        def body(step, acc, group=group, used=used):
            values = {}
            for k in used:
                for part in range(2):
                    v = block(step, k, part)
                    high = (v + grids[k]) - grids[k]
                    values[k, part] = v, high, v - high

            def products(a, b):
                return a[1] * b[1], a[1] * b[2] + a[2] * b[0]

            new = []
            for i, j in group:
                x, y = products(values[i, 0], values[j, 0]), products(values[i, 1], values[j, 1])
                re = acc[len(new)]
                new.append(tuple(re[n] + (x[n] + y[n]) for n in range(2)))
                if i != j:
                    x, y = products(values[i, 0], values[j, 1]), products(values[i, 1], values[j, 0])
                    im = acc[len(new)]
                    new.append(tuple(im[n] + (x[n] - y[n]) for n in range(2)))
            return tuple(new)

        sums += list(
            lax.fori_loop(0, 24, body, tuple((zero, zero) for _ in range(count)), unroll=6)
        )
    count = len(sums)
    for k, s in enumerate(sums):
        for n in range(2):
            spare[n, 8 * k : 8 * k + 8, :] = s[n]
    lines = [tuple(spare[n, pl.ds(row, count, stride=8), :] for n in range(2)) for row in range(8)]
    while len(lines) > 1:
        lines = [pair_add(x, y) for x, y in zip(lines[::2], lines[1::2])]
    s = lines[0]
    for shift in (64, 32, 16, 8, 4, 2, 1):
        s = pair_add(s, tuple(pltpu.roll(v, shift, 1) for v in s))
    away = iota(s[0].shape, 1) - iota(s[0].shape, 0)
    line = jnp.where(away == 0, s[0], F32(0)) + jnp.where(away == 64, s[1], F32(0))
    line = jnp.sum(line, axis=0, keepdims=True)
    out[...] = jnp.broadcast_to(line, out.shape)


def gathered(parts, pairs):
    lines = []
    for n in range(parts.shape[0] // 8):
        high = parts[8 * n : 8 * n + 8, :]
        lines.append((high, pltpu.roll(high, 64, 1)))
    s = total(lines)
    for shift in (4, 2, 1):
        s = pair_add(s, tuple(pltpu.roll(v, shift, 0) for v in s))
    entries, at = {}, 0

    def lane(k):
        return tuple(jnp.broadcast_to(v[:, k : k + 1], BLK) for v in s)

    zero = (jnp.zeros(BLK, F32), jnp.zeros(BLK, F32))
    for i, j in pairs:
        re, at = lane(at), at + 1
        im = zero
        if i != j:
            im, at = lane(at), at + 1
        entries[i, j] = (re, im)
        entries[j, i] = (re, negate(im)) if i != j else (re, im)
    return entries


def rows(v):
    return tuple(jnp.concatenate([x] * (ROWS // 8), axis=0) for x in v)


def scaled(v, re, im):
    return v[0] * re - v[1] * im, v[0] * im + v[1] * re


PAIRS_1 = ((1, 1), (2, 2), (0, 1), (1, 2), (0, 2))
PAIRS_2 = ((1, 1), (2, 2), (3, 3), (4, 4), (0, 1), (0, 2), (1, 2), (0, 3), (0, 4), (1, 3), (1, 4), (2, 3), (2, 4), (3, 4))


def place_measurements(me, n_slabs, slab_of, cell_of, comp_of, ranks, hot_z, hot_row):
    upper = (iota((LANES, LANES), 0) <= iota((LANES, LANES), 1)).astype(jnp.bfloat16)
    key = (comp_of[...] * 8192 + cell_of[...]).astype(F32)
    n_blocks = key.shape[0]
    slots = n_blocks * CAP
    same = (iota((slots, slots), 0) == iota((slots, slots), 1)).astype(jnp.bfloat16)

    @pl.loop(0, len(SLABS), unroll=6)
    def _(s):
        slab = lax.rem(me + s + SLABS[0] + n_slabs, n_slabs)
        mine = slab_of[...] == slab
        mine_f = jnp.where(mine, F32(1), F32(0))
        rank = jnp.dot(mine_f.astype(jnp.bfloat16), upper, preferred_element_type=F32)
        rank = jnp.where(mine, rank, F32(0))
        ranks[s] = rank
        place = column(rank, key).astype(jnp.int32)
        at_z = (place & (LANES - 1)) == iota((slots, LANES), 1)
        hot_z[s] = jnp.where(at_z, F32(1), F32(0))
        at_row = jnp.where((place >> 7) == iota((slots, 256), 1), F32(1), F32(0))
        turned = lax.dot_general(
            at_row.astype(jnp.bfloat16), same, (((0,), (0,)), ((), ())), preferred_element_type=F32
        )
        hot_row[s] = turned.astype(jnp.bfloat16)


def column(rank, values):
    n_blocks = rank.shape[0]
    slot = (iota((n_blocks, CAP, LANES), 1) + 1).astype(F32)
    v = jnp.where(rank[:, None, :] == slot, values[:, None, :], F32(0))
    return jnp.sum(v, axis=2, keepdims=True).reshape(n_blocks * CAP, 1)


def scatter_source(weights, ranks, hot_z, hot_row, source):
    @pl.loop(0, len(SLABS), unroll=len(SLABS))
    def _(s):
        put = jnp.concatenate(
            [hot_z[s] * column(ranks[s], weights[:, part, :]) for part in range(2)], axis=1
        )
        grid = None
        for _ in range(3):
            piece = put.astype(jnp.bfloat16)
            put = put - piece.astype(F32)
            term = jnp.dot(hot_row[s], piece, preferred_element_type=F32)
            grid = term if grid is None else grid + term
        for part in range(2):
            for comp in range(3):
                for plane in range(2):
                    row = comp * 64 + plane * 32
                    source[3 * part + comp, 2 * s + plane] = grid[
                        row : row + 32, part * LANES : (part + 1) * LANES
                    ]


def into(ref):
    def store(part, comp, at, value):
        ref[3 * part + comp, at] = value

    return store


def place_kernel(
    n_slabs, slab_of, cell_of, comp_of, freqs, pair, ranks, hot_z, hot_row, wave
):
    me = lax.axis_index("space")
    wave[...] = jnp.full(BLK, freqs[pair[0]], F32)
    place_measurements(me, n_slabs, slab_of, cell_of, comp_of, ranks, hot_z, hot_row)


def start_kernel(
    own, b2, b1, a1, a2, a3, weights, ranks, hot_z, hot_row, wave,
    p0_out, p1_out, p2_out, damp_out, gram_out,
    field, damping, source, p0, p1, spare,
):
    me = lax.axis_index("space")
    for s, ref in enumerate((b2, b1, own, a1, a2, a3)):
        for k in range(6):
            field[k, 2 * s : 2 * s + 2] = ref[2 * k : 2 * k + 2]
        damping[2 * s : 2 * s + 2] = ref[12:14] * wave[0:1, :]
    scatter_source(weights, ranks, hot_z, hot_row, source)

    def keep_p0(part, comp, at, value):
        p0[3 * part + comp, at] = source[3 * part + comp, at] - value

    def keep_p2(part, comp, at, value):
        p2_out[3 * part + comp, at - 3] = value

    apply(me, field, damping, -4, 1, 11, keep_p0, 5)
    apply(me, p0, damping, -4, 2, 10, into(p1), 4)
    apply(me, p1, damping, -4, 3, 9, keep_p2, 3)
    for k in range(6):
        p0_out[k] = p0[k, 3:9]
        p1_out[k] = p1[k, 3:9]
    damp_out[...] = damping[3:9]
    gram(((p0, 5), (p1, 5), (p2_out, 2)), PAIRS_1, gram_out, spare)


def middle_kernel(
    parts, p0, p1, p2, damping, own,
    xs_out, r_out, d_out, m_out, f_out, gram_out,
    r, m, f, g, h, spare,
):
    me = lax.axis_index("space")
    e = gathered(parts, PAIRS_1)
    den = e[1, 1][0][0]
    a = over(e[1, 0], den)
    t = csum([e[1, 1], mix(e[1, 2], cneg(a))])
    b = cneg(over(t, den))
    u = (F32(1) + b[0], b[1])
    w = [conj(csum([mix(e[i, 1], u), mix(e[i, 2], cneg(a))])) for i in range(3)]
    num = csum([w[0], mix(w[1], cneg(a))])
    den = pair_add(mix_re(w[1], u), mix_re(w[2], cneg(a)))[0]
    step = over(num, den)
    su = cmul(step, u)
    s = (a[0] + su[0], a[1] + su[1])
    v = cmul(step, a)
    a, u, s, v = rows(a), rows(u), rows(s), rows(v)

    @pl.loop(0, 6)
    def _(at):
        for c in range(3):
            v0 = (p0[c, at], p0[3 + c, at])
            v1 = (p1[c, at], p1[3 + c, at])
            v2 = (p2[c, at], p2[3 + c, at])
            s1, w2 = scaled(s, *v1), scaled(v, *v2)
            u1, a2 = scaled(u, *v1), scaled(a, *v2)
            for part in range(2):
                r[3 * part + c, at] = (v0[part] - s1[part]) + w2[part]
                m[3 * part + c, at] = u1[part] - a2[part]

    for plane in range(2):
        for c in range(3):
            v0 = (p0[c, 1 + plane], p0[3 + c, 1 + plane])
            v1 = (p1[c, 1 + plane], p1[3 + c, 1 + plane])
            s0, w1 = scaled(s, *v0), scaled(v, *v1)
            u0, a1 = scaled(u, *v0), scaled(a, *v1)
            for part in range(2):
                k = 2 * (3 * part + c) + plane
                xs_out[k] = (own[k] + s0[part]) - w1[part]
                d_out[k] = u0[part] - a1[part]
                r_out[k] = r[3 * part + c, 1 + plane]
                m_out[k] = m[3 * part + c, 1 + plane]

    apply(me, r, damping, -1, 1, 5, into(f))
    apply(me, m, damping, -1, 2, 4, into(g))
    apply(me, f, damping, -1, 2, 4, into(h))
    for k in range(6):
        f_out[2 * k : 2 * k + 2] = f[k, 1:3]
    gram(((r, 2), (m, 2), (f, 2), (g, 2), (h, 2)), PAIRS_2, gram_out, spare)


def end_kernel(parts, xs, r, d, m, f, background, wave, adjoint_out, terms_out):
    e = gathered(parts, PAIRS_2)
    b = cneg(over(e[1, 2], e[1, 1][0][0]))
    w = [conj(csum([mix(e[i, 1], b), e[i, 2]])) for i in range(5)]
    den = pair_add(mix_re(w[1], b), w[2][0])[0]
    a = over(w[0], den)
    ab = cmul(a, b)
    t = csum([w[2], mix(w[3], cneg(ab)), mix(w[4], cneg(a))])
    b2 = cneg(over(t, den))
    q1, q2 = (F32(1) + b2[0], b2[1]), cmul(b2, b)
    mapped = (q2, q1, cneg(ab), cneg(a))
    w = [conj(csum([mix(e[i, 1 + k], q) for k, q in enumerate(mapped)])) for i in range(5)]
    num = csum([w[0], mix(w[1], cneg(ab)), mix(w[2], cneg(a))])
    den = total([mix_re(w[1 + k], q) for k, q in enumerate(mapped)])[0]
    a2 = over(num, den)
    to_r, to_d = cmul(a2, q1), cmul(a2, q2)
    to_r = rows((a[0] + to_r[0], a[1] + to_r[1]))
    to_d = rows((ab[0] + to_d[0], ab[1] + to_d[1]))
    to_f, to_m = rows(cmul(a2, a)), rows(cmul(a2, ab))
    for plane in range(2):
        terms = jnp.zeros((ROWS, LANES), F32)
        for c in range(3):
            k, q = 2 * c + plane, 2 * (3 + c) + plane
            add = [
                scaled(to_r, r[k], r[q]),
                scaled(to_d, d[k], d[q]),
                cneg(scaled(to_f, f[k], f[q])),
                cneg(scaled(to_m, m[k], m[q])),
            ]
            re = xs[k] + ((add[0][0] + add[1][0]) + (add[2][0] + add[3][0]))
            im = xs[q] + ((add[0][1] + add[1][1]) + (add[2][1] + add[3][1]))
            adjoint_out[k] = re
            adjoint_out[q] = im
            terms = terms + (re * background[q] + im * background[k])
        terms = terms * wave[0:1, :]
        n_src = terms_out.shape[0]
        part = ROWS // n_src
        for n in range(n_src):
            terms_out[n, plane * part : (plane + 1) * part] = terms[n * part : (n + 1) * part]


def shaped(*shape):
    return jax.ShapeDtypeStruct(shape, F32)


def kernel(body, name, in_specs, outs, scratch, flops):
    return pl.pallas_call(
        body,
        name=name,
        in_specs=in_specs,
        out_specs=tuple(spec() for _ in outs),
        out_shape=tuple(outs),
        scratch_shapes=[pltpu.VMEM(s, F32) for s in scratch],
        compiler_params=pltpu.CompilerParams(vmem_limit_bytes=VMEM_BYTES),
        cost_estimate=pl.CostEstimate(flops=flops, bytes_accessed=3_000_000, transcendentals=0),
    )


def shards(
    background,
    warm_start,
    conductivity,
    frequencies,
    pair_freq,
    weighted_residual,
    datum_layer_index,
    receiver_flat_cell,
    receiver_component,
):
    n_slabs, n_src = lax.axis_size("space"), lax.axis_size("src")
    own = warm_start.reshape(12, ROWS, LANES)
    message = jnp.concatenate([own, conductivity], axis=0)

    def from_slab(away):
        route = [((i + away) % n_slabs, i) for i in range(n_slabs)]
        return lax.ppermute(message, "space", route)

    window = [from_slab(away) for away in (-2, -1, 1, 2, 3)]
    weights = jnp.broadcast_to(weighted_residual.reshape(1, 2, LANES), (n_slabs, 2, LANES))
    weights = lax.all_to_all(weights, "space", split_axis=0, concat_axis=0, tiled=True)
    plane = (ROWS, LANES)
    slab_of = datum_layer_index.reshape(n_slabs, LANES)
    cell_of = receiver_flat_cell.reshape(n_slabs, LANES)
    comp_of = receiver_component.reshape(n_slabs, LANES)
    smem = spec(pltpu.SMEM)
    six = shaped(6, 6, *plane)
    slots = n_slabs * CAP
    places = kernel(
        functools.partial(place_kernel, n_slabs),
        "place",
        [spec()] * 3 + [smem] * 2,
        [
            shaped(len(SLABS), *plane),
            shaped(len(SLABS), slots, LANES),
            jax.ShapeDtypeStruct((len(SLABS), 256, slots), jnp.bfloat16),
            shaped(*BLK),
        ],
        [],
        20_000_000,
    )(slab_of, cell_of, comp_of, frequencies, pair_freq)
    wave = places[-1]
    p0, p1, p2, damping, parts = kernel(
        start_kernel,
        "start",
        [spec()] * 11,
        [six, six, six, shaped(6, *plane), shaped(n_slabs, LANES)],
        [(6, 12, *plane), (12, *plane), *[(6, 12, *plane)] * 3, (2, 64, LANES)],
        40_000_000,
    )(message, *window, weights, *places)
    parts = lax.all_to_all(parts, "space", split_axis=0, concat_axis=0, tiled=True)
    two = shaped(12, *plane)
    xs, r, d, m, f, parts = kernel(
        middle_kernel,
        "middle",
        [spec()] * 6,
        [two] * 5 + [shaped(n_slabs, LANES)],
        [(6, 6, *plane)] * 5 + [(2, 192, LANES)],
        40_000_000,
    )(parts, p0, p1, p2, damping, own)
    parts = lax.all_to_all(parts, "space", split_axis=0, concat_axis=0, tiled=True)
    adjoint, terms = kernel(
        end_kernel,
        "end",
        [spec()] * 8,
        [two, shaped(n_src, 2 * (ROWS // n_src), LANES)],
        [],
        5_000_000,
    )(parts, xs, r, d, m, f, background.reshape(12, *plane), wave)
    terms = lax.all_to_all(terms, "src", split_axis=0, concat_axis=0, tiled=True)
    gradient = jnp.sum(terms, axis=0).reshape(2, ROWS // n_src, LANES)
    return adjoint.reshape(warm_start.shape), gradient


def solution(mesh):
    placed = (
        P(None, "src", None, "space", None, None),
        P(None, "src", None, "space", None, None),
        P("space", None, None),
        P(),
        P("src"),
        P(None, "src", "space"),
        P(),
        P(),
        P(),
    )
    return jax.shard_map(
        shards,
        mesh=mesh,
        in_specs=placed,
        out_specs=(P(None, "src", None, "space", None, None), P("space", "src", None)),
        check_vma=False,
    )
```

```python
import functools

import jax
import jax.numpy as jnp
from jax import lax
from jax.experimental import pallas as pl
from jax.experimental.pallas import tpu as pltpu
from jax.sharding import PartitionSpec as P

F32 = jnp.float32
SLABS = (-2, -1, 0, 1, 2, 3)
ROWS, LANES = 32, 128
BLK = (8, 128)
CAP = 8
VMEM_BYTES = 14 * 1024 * 1024


def spec(space=pltpu.VMEM):
    return pl.BlockSpec(memory_space=space)


def iota(shape, axis):
    return lax.broadcasted_iota(jnp.int32, shape, axis)


def two_sum(a, b):
    s = a + b
    t = s - a
    return s, (a - (s - t)) + (b - t)


def split(a):
    t = a * F32(4097.0)
    high = t - (t - a)
    return high, a - high


def product_error(p, a, b):
    (ah, al), (bh, bl) = a, b
    return ((ah * bh - p) + ah * bl + al * bh) + al * bl


def pair_add(a, b):
    s, e = two_sum(a[0], b[0])
    e = e + (a[1] + b[1])
    h = s + e
    return h, e - (h - s)


def pair_scale(a, c):
    p = a[0] * c
    e = product_error(p, split(a[0]), split(c)) + a[1] * c
    h = p + e
    return h, e - (h - p)


def negate(a):
    return tuple(-v for v in a)


def total(terms):
    terms = list(terms)
    while len(terms) > 1:
        terms = [pair_add(x, y) for x, y in zip(terms[::2], terms[1::2])] + terms[len(terms) // 2 * 2 :]
    return terms[0]


def mix_re(g, v):
    return pair_add(pair_scale(g[0], v[0]), negate(pair_scale(g[1], v[1])))


def mix(g, v):
    return mix_re(g, v), pair_add(pair_scale(g[0], v[1]), pair_scale(g[1], v[0]))


def csum(terms):
    return total([t[0] for t in terms]), total([t[1] for t in terms])


def conj(g):
    return g[0], negate(g[1])


def cneg(v):
    return -v[0], -v[1]


def cmul(a, b):
    return a[0] * b[0] - a[1] * b[1], a[0] * b[1] + a[1] * b[0]


def over(g, den):
    return g[0][0] / den, g[1][0] / den


def y_next(e):
    return jnp.where(iota(e.shape, 0) == ROWS - 1, F32(0), pltpu.roll(e, ROWS - 1, 0))


def z_next(e):
    return jnp.where(iota(e.shape, 1) == LANES - 1, F32(0), pltpu.roll(e, LANES - 1, 1))


def y_prev(h, first):
    return jnp.where(iota(h.shape, 0) == 0, first, pltpu.roll(h, 1, 0))


def z_prev(h, first):
    return jnp.where(iota(h.shape, 1) == 0, first, pltpu.roll(h, 1, 1))


def forward_yz(ex, ey, ez, ey_up, ez_up):
    hy = (z_next(ex) - ex) - (ez_up - ez)
    hz = (ey_up - ey) - (y_next(ex) - ex)
    return hy, hz


def curl_curl(field, part, at, above, below, before):
    ex, ey, ez = (field[3 * part + c, at] for c in range(3))
    ey_up, ez_up = (field[3 * part + c, at + 1] * above for c in (1, 2))
    hx = (y_next(ez) - ez) - (z_next(ey) - ey)
    hy, hz = forward_yz(ex, ey, ez, ey_up, ez_up)
    edge = F32(1) - below
    hy_dn = before[0] * below - ez * edge
    hz_dn = before[1] * below + ey * edge
    result = (
        (hz - y_prev(hz, -ex)) - (hy - z_prev(hy, ex)),
        (hx - z_prev(hx, -ey)) - (hz - hz_dn),
        (hy - hy_dn) - (hx - y_prev(hx, ez)),
    )
    return result, (hy, hz)


def apply(me, field, damping, first, low, high, store, unroll=2):
    def plane(at, before):
        grid_plane = lax.rem(2 * me + first + at + 64, 64)
        above = jnp.where(grid_plane == 63, F32(0), F32(1))
        below = jnp.where(grid_plane == 0, F32(0), F32(1))
        damp = damping[at]
        real, real_h = curl_curl(field, 0, at, above, below, before[:2])
        for c in range(3):
            store(0, c, at, real[c] - damp * field[3 + c, at])
        imag, imag_h = curl_curl(field, 1, at, above, below, before[2:])
        for c in range(3):
            store(1, c, at, imag[c] + damp * field[c, at])
        return real_h + imag_h

    below_first = []
    for part in range(2):
        under = [field[3 * part + c, low - 1] for c in range(3)]
        below_first += forward_yz(*under, *(field[3 * part + c, low] for c in (1, 2)))
    lax.fori_loop(low, high, plane, tuple(below_first), unroll=unroll)


def gram(fields, pairs, out, spare, size=14):
    names = sorted({k for pair in pairs for k in pair})

    def block(step, k, part):
        comp, rest = step // 8, lax.rem(step, 8)
        plane, row = rest // 4, pl.multiple_of(lax.rem(rest, 4) * 8, 8)
        ref, start = fields[k]
        return ref[3 * part + comp, start + plane, pl.ds(row, 8), :]

    def peak(step, tops):
        return tuple(
            jnp.maximum(top, jnp.maximum(jnp.abs(block(step, k, 0)), jnp.abs(block(step, k, 1))))
            for k, top in zip(names, tops)
        )

    zero = jnp.zeros(BLK, F32)
    tops = lax.fori_loop(0, 24, peak, tuple(zero for _ in names), unroll=6)
    grids = {k: top * F32(2.0**15) for k, top in zip(names, tops)}
    sums = []
    for first in range(0, len(pairs), size):
        group = pairs[first : first + size]
        used = sorted({k for pair in group for k in pair})
        count = sum(1 if i == j else 2 for i, j in group)

        def body(step, acc, group=group, used=used):
            values = {}
            for k in used:
                for part in range(2):
                    v = block(step, k, part)
                    high = (v + grids[k]) - grids[k]
                    values[k, part] = v, high, v - high

            def products(a, b):
                return a[1] * b[1], a[1] * b[2] + a[2] * b[0]

            new = []
            for i, j in group:
                x, y = products(values[i, 0], values[j, 0]), products(values[i, 1], values[j, 1])
                re = acc[len(new)]
                new.append(tuple(re[n] + (x[n] + y[n]) for n in range(2)))
                if i != j:
                    x, y = products(values[i, 0], values[j, 1]), products(values[i, 1], values[j, 0])
                    im = acc[len(new)]
                    new.append(tuple(im[n] + (x[n] - y[n]) for n in range(2)))
            return tuple(new)

        sums += list(
            lax.fori_loop(0, 24, body, tuple((zero, zero) for _ in range(count)), unroll=6)
        )
    count = len(sums)
    for k, s in enumerate(sums):
        for n in range(2):
            spare[n, 8 * k : 8 * k + 8, :] = s[n]
    lines = [tuple(spare[n, pl.ds(row, count, stride=8), :] for n in range(2)) for row in range(8)]
    while len(lines) > 1:
        lines = [pair_add(x, y) for x, y in zip(lines[::2], lines[1::2])]
    s = lines[0]
    for shift in (64, 32, 16, 8, 4, 2, 1):
        s = pair_add(s, tuple(pltpu.roll(v, shift, 1) for v in s))
    away = iota(s[0].shape, 1) - iota(s[0].shape, 0)
    line = jnp.where(away == 0, s[0], F32(0)) + jnp.where(away == 64, s[1], F32(0))
    line = jnp.sum(line, axis=0, keepdims=True)
    out[...] = jnp.broadcast_to(line, out.shape)


def gathered(parts, pairs):
    lines = []
    for n in range(parts.shape[0] // 8):
        high = parts[8 * n : 8 * n + 8, :]
        lines.append((high, pltpu.roll(high, 64, 1)))
    s = total(lines)
    for shift in (4, 2, 1):
        s = pair_add(s, tuple(pltpu.roll(v, shift, 0) for v in s))
    entries, at = {}, 0

    def lane(k):
        return tuple(jnp.broadcast_to(v[:, k : k + 1], BLK) for v in s)

    zero = (jnp.zeros(BLK, F32), jnp.zeros(BLK, F32))
    for i, j in pairs:
        re, at = lane(at), at + 1
        im = zero
        if i != j:
            im, at = lane(at), at + 1
        entries[i, j] = (re, im)
        entries[j, i] = (re, negate(im)) if i != j else (re, im)
    return entries


def rows(v):
    return tuple(jnp.concatenate([x] * (ROWS // 8), axis=0) for x in v)


def scaled(v, re, im):
    return v[0] * re - v[1] * im, v[0] * im + v[1] * re


PAIRS_1 = ((1, 1), (2, 2), (0, 1), (1, 2), (0, 2))
PAIRS_2 = ((1, 1), (2, 2), (3, 3), (4, 4), (0, 1), (0, 2), (1, 2), (0, 3), (0, 4), (1, 3), (1, 4), (2, 3), (2, 4), (3, 4))


def place_measurements(me, n_slabs, slab_of, cell_of, comp_of, ranks, hot_z, hot_row):
    upper = (iota((LANES, LANES), 0) <= iota((LANES, LANES), 1)).astype(jnp.bfloat16)
    key = (comp_of[...] * 8192 + cell_of[...]).astype(F32)
    n_blocks = key.shape[0]
    slots = n_blocks * CAP
    same = (iota((slots, slots), 0) == iota((slots, slots), 1)).astype(jnp.bfloat16)

    @pl.loop(0, len(SLABS), unroll=6)
    def _(s):
        slab = lax.rem(me + s + SLABS[0] + n_slabs, n_slabs)
        mine = slab_of[...] == slab
        mine_f = jnp.where(mine, F32(1), F32(0))
        rank = jnp.dot(mine_f.astype(jnp.bfloat16), upper, preferred_element_type=F32)
        rank = jnp.where(mine, rank, F32(0))
        ranks[s] = rank
        place = column(rank, key).astype(jnp.int32)
        at_z = (place & (LANES - 1)) == iota((slots, LANES), 1)
        hot_z[s] = jnp.where(at_z, F32(1), F32(0))
        at_row = jnp.where((place >> 7) == iota((slots, 256), 1), F32(1), F32(0))
        turned = lax.dot_general(
            at_row.astype(jnp.bfloat16), same, (((0,), (0,)), ((), ())), preferred_element_type=F32
        )
        hot_row[s] = turned.astype(jnp.bfloat16)


def column(rank, values):
    n_blocks = rank.shape[0]
    slot = (iota((n_blocks, CAP, LANES), 1) + 1).astype(F32)
    v = jnp.where(rank[:, None, :] == slot, values[:, None, :], F32(0))
    return jnp.sum(v, axis=2, keepdims=True).reshape(n_blocks * CAP, 1)


def scatter_source(weights, ranks, hot_z, hot_row, source):
    @pl.loop(0, len(SLABS), unroll=len(SLABS))
    def _(s):
        put = jnp.concatenate(
            [hot_z[s] * column(ranks[s], weights[:, part, :]) for part in range(2)], axis=1
        )
        grid = None
        for _ in range(3):
            piece = put.astype(jnp.bfloat16)
            put = put - piece.astype(F32)
            term = jnp.dot(hot_row[s], piece, preferred_element_type=F32)
            grid = term if grid is None else grid + term
        for part in range(2):
            for comp in range(3):
                for plane in range(2):
                    row = comp * 64 + plane * 32
                    source[3 * part + comp, 2 * s + plane] = grid[
                        row : row + 32, part * LANES : (part + 1) * LANES
                    ]


def into(ref):
    def store(part, comp, at, value):
        ref[3 * part + comp, at] = value

    return store


def place_kernel(
    n_slabs, slab_of, cell_of, comp_of, freqs, pair, ranks, hot_z, hot_row, wave
):
    me = lax.axis_index("space")
    wave[...] = jnp.full(BLK, freqs[pair[0]], F32)
    place_measurements(me, n_slabs, slab_of, cell_of, comp_of, ranks, hot_z, hot_row)


def start_kernel(
    own, b2, b1, a1, a2, a3, weights, ranks, hot_z, hot_row, wave,
    p0_out, p1_out, p2_out, damp_out, gram_out,
    field, damping, source, p0, p1, spare,
):
    me = lax.axis_index("space")
    for s, ref in enumerate((b2, b1, own, a1, a2, a3)):
        for k in range(6):
            field[k, 2 * s : 2 * s + 2] = ref[2 * k : 2 * k + 2]
        damping[2 * s : 2 * s + 2] = ref[12:14] * wave[0:1, :]
    scatter_source(weights, ranks, hot_z, hot_row, source)

    def keep_p0(part, comp, at, value):
        p0[3 * part + comp, at] = source[3 * part + comp, at] - value

    def keep_p2(part, comp, at, value):
        p2_out[3 * part + comp, at - 3] = value

    apply(me, field, damping, -4, 1, 11, keep_p0, 5)
    apply(me, p0, damping, -4, 2, 10, into(p1), 4)
    apply(me, p1, damping, -4, 3, 9, keep_p2, 3)
    for k in range(6):
        p0_out[k] = p0[k, 3:9]
        p1_out[k] = p1[k, 3:9]
    damp_out[...] = damping[3:9]
    gram(((p0, 5), (p1, 5), (p2_out, 2)), PAIRS_1, gram_out, spare)


def middle_kernel(
    parts, p0, p1, p2, damping, own,
    xs_out, r_out, d_out, m_out, f_out, gram_out,
    r, m, f, g, h, spare,
):
    me = lax.axis_index("space")
    e = gathered(parts, PAIRS_1)
    den = e[1, 1][0][0]
    a = over(e[1, 0], den)
    t = csum([e[1, 1], mix(e[1, 2], cneg(a))])
    b = cneg(over(t, den))
    u = (F32(1) + b[0], b[1])
    w = [conj(csum([mix(e[i, 1], u), mix(e[i, 2], cneg(a))])) for i in range(3)]
    num = csum([w[0], mix(w[1], cneg(a))])
    den = pair_add(mix_re(w[1], u), mix_re(w[2], cneg(a)))[0]
    step = over(num, den)
    su = cmul(step, u)
    s = (a[0] + su[0], a[1] + su[1])
    v = cmul(step, a)
    a, u, s, v = rows(a), rows(u), rows(s), rows(v)

    @pl.loop(0, 6, unroll=3)
    def _(at):
        for c in range(3):
            v0 = (p0[c, at], p0[3 + c, at])
            v1 = (p1[c, at], p1[3 + c, at])
            v2 = (p2[c, at], p2[3 + c, at])
            s1, w2 = scaled(s, *v1), scaled(v, *v2)
            u1, a2 = scaled(u, *v1), scaled(a, *v2)
            for part in range(2):
                r[3 * part + c, at] = (v0[part] - s1[part]) + w2[part]
                m[3 * part + c, at] = u1[part] - a2[part]

    for plane in range(2):
        for c in range(3):
            v0 = (p0[c, 1 + plane], p0[3 + c, 1 + plane])
            v1 = (p1[c, 1 + plane], p1[3 + c, 1 + plane])
            s0, w1 = scaled(s, *v0), scaled(v, *v1)
            u0, a1 = scaled(u, *v0), scaled(a, *v1)
            for part in range(2):
                k = 2 * (3 * part + c) + plane
                xs_out[k] = (own[k] + s0[part]) - w1[part]
                d_out[k] = u0[part] - a1[part]
                r_out[k] = r[3 * part + c, 1 + plane]
                m_out[k] = m[3 * part + c, 1 + plane]

    apply(me, r, damping, -1, 1, 5, into(f))
    apply(me, m, damping, -1, 2, 4, into(g))
    apply(me, f, damping, -1, 2, 4, into(h))
    for k in range(6):
        f_out[2 * k : 2 * k + 2] = f[k, 1:3]
    gram(((r, 2), (m, 2), (f, 2), (g, 2), (h, 2)), PAIRS_2, gram_out, spare)


def end_kernel(parts, xs, r, d, m, f, background, wave, adjoint_out, terms_out):
    e = gathered(parts, PAIRS_2)
    b = cneg(over(e[1, 2], e[1, 1][0][0]))
    w = [conj(csum([mix(e[i, 1], b), e[i, 2]])) for i in range(5)]
    den = pair_add(mix_re(w[1], b), w[2][0])[0]
    a = over(w[0], den)
    ab = cmul(a, b)
    t = csum([w[2], mix(w[3], cneg(ab)), mix(w[4], cneg(a))])
    b2 = cneg(over(t, den))
    q1, q2 = (F32(1) + b2[0], b2[1]), cmul(b2, b)
    mapped = (q2, q1, cneg(ab), cneg(a))
    w = [conj(csum([mix(e[i, 1 + k], q) for k, q in enumerate(mapped)])) for i in range(5)]
    num = csum([w[0], mix(w[1], cneg(ab)), mix(w[2], cneg(a))])
    den = total([mix_re(w[1 + k], q) for k, q in enumerate(mapped)])[0]
    a2 = over(num, den)
    to_r, to_d = cmul(a2, q1), cmul(a2, q2)
    to_r = rows((a[0] + to_r[0], a[1] + to_r[1]))
    to_d = rows((ab[0] + to_d[0], ab[1] + to_d[1]))
    to_f, to_m = rows(cmul(a2, a)), rows(cmul(a2, ab))
    for plane in range(2):
        terms = jnp.zeros((ROWS, LANES), F32)
        for c in range(3):
            k, q = 2 * c + plane, 2 * (3 + c) + plane
            add = [
                scaled(to_r, r[k], r[q]),
                scaled(to_d, d[k], d[q]),
                cneg(scaled(to_f, f[k], f[q])),
                cneg(scaled(to_m, m[k], m[q])),
            ]
            re = xs[k] + ((add[0][0] + add[1][0]) + (add[2][0] + add[3][0]))
            im = xs[q] + ((add[0][1] + add[1][1]) + (add[2][1] + add[3][1]))
            adjoint_out[k] = re
            adjoint_out[q] = im
            terms = terms + (re * background[q] + im * background[k])
        terms = terms * wave[0:1, :]
        n_src = terms_out.shape[0]
        part = ROWS // n_src
        for n in range(n_src):
            terms_out[n, plane * part : (plane + 1) * part] = terms[n * part : (n + 1) * part]


def shaped(*shape):
    return jax.ShapeDtypeStruct(shape, F32)


def kernel(body, name, in_specs, outs, scratch, flops):
    return pl.pallas_call(
        body,
        name=name,
        in_specs=in_specs,
        out_specs=tuple(spec() for _ in outs),
        out_shape=tuple(outs),
        scratch_shapes=[pltpu.VMEM(s, F32) for s in scratch],
        compiler_params=pltpu.CompilerParams(vmem_limit_bytes=VMEM_BYTES),
        cost_estimate=pl.CostEstimate(flops=flops, bytes_accessed=3_000_000, transcendentals=0),
    )


def shards(
    background,
    warm_start,
    conductivity,
    frequencies,
    pair_freq,
    weighted_residual,
    datum_layer_index,
    receiver_flat_cell,
    receiver_component,
):
    n_slabs, n_src = lax.axis_size("space"), lax.axis_size("src")
    own = warm_start.reshape(12, ROWS, LANES)
    message = jnp.concatenate([own, conductivity], axis=0)

    def from_slab(away):
        route = [((i + away) % n_slabs, i) for i in range(n_slabs)]
        return lax.ppermute(message, "space", route)

    window = [from_slab(away) for away in (-2, -1, 1, 2, 3)]
    weights = jnp.broadcast_to(weighted_residual.reshape(1, 2, LANES), (n_slabs, 2, LANES))
    weights = lax.all_to_all(weights, "space", split_axis=0, concat_axis=0, tiled=True)
    plane = (ROWS, LANES)
    slab_of = datum_layer_index.reshape(n_slabs, LANES)
    cell_of = receiver_flat_cell.reshape(n_slabs, LANES)
    comp_of = receiver_component.reshape(n_slabs, LANES)
    smem = spec(pltpu.SMEM)
    six = shaped(6, 6, *plane)
    slots = n_slabs * CAP
    places = kernel(
        functools.partial(place_kernel, n_slabs),
        "place",
        [spec()] * 3 + [smem] * 2,
        [
            shaped(len(SLABS), *plane),
            shaped(len(SLABS), slots, LANES),
            jax.ShapeDtypeStruct((len(SLABS), 256, slots), jnp.bfloat16),
            shaped(*BLK),
        ],
        [],
        20_000_000,
    )(slab_of, cell_of, comp_of, frequencies, pair_freq)
    wave = places[-1]
    p0, p1, p2, damping, parts = kernel(
        start_kernel,
        "start",
        [spec()] * 11,
        [six, six, six, shaped(6, *plane), shaped(n_slabs, LANES)],
        [(6, 12, *plane), (12, *plane), *[(6, 12, *plane)] * 3, (2, 64, LANES)],
        40_000_000,
    )(message, *window, weights, *places)
    parts = lax.all_to_all(parts, "space", split_axis=0, concat_axis=0, tiled=True)
    two = shaped(12, *plane)
    xs, r, d, m, f, parts = kernel(
        middle_kernel,
        "middle",
        [spec()] * 6,
        [two] * 5 + [shaped(n_slabs, LANES)],
        [(6, 6, *plane)] * 5 + [(2, 192, LANES)],
        40_000_000,
    )(parts, p0, p1, p2, damping, own)
    parts = lax.all_to_all(parts, "space", split_axis=0, concat_axis=0, tiled=True)
    adjoint, terms = kernel(
        end_kernel,
        "end",
        [spec()] * 8,
        [two, shaped(n_src, 2 * (ROWS // n_src), LANES)],
        [],
        5_000_000,
    )(parts, xs, r, d, m, f, background.reshape(12, *plane), wave)
    terms = lax.all_to_all(terms, "src", split_axis=0, concat_axis=0, tiled=True)
    gradient = jnp.sum(terms, axis=0).reshape(2, ROWS // n_src, LANES)
    return adjoint.reshape(warm_start.shape), gradient


def solution(mesh):
    placed = (
        P(None, "src", None, "space", None, None),
        P(None, "src", None, "space", None, None),
        P("space", None, None),
        P(),
        P("src"),
        P(None, "src", "space"),
        P(),
        P(),
        P(),
    )
    return jax.shard_map(
        shards,
        mesh=mesh,
        in_specs=placed,
        out_specs=(P(None, "src", None, "space", None, None), P("space", "src", None)),
        check_vma=False,
    )
```
